32 devices in a mesh: groups: 2 (over y), ctx: 4 (over z), head: 4 (over x, core).
Axes of the slice: x: 2, y: 2, z: 4, core: 2. Of those that a mesh axis runs over, the one named last changes fastest.
Arguments:
- tokens: bfloat16 [4096, 4096], P(('groups', 'ctx')), parts along dimension 0, may hold values from -14 to 14
- lengths: int32 [32], P('groups'), parts along dimension 0, may hold values from 1 to 1024, 2048 in all
- q_weight: bfloat16 [4096, 4096], P(None, 'head'), may hold values from -21 to 21
- k_weight: bfloat16 [4096, 1024], P(None, 'head'), may hold values from -7 to 7
- v_weight: bfloat16 [4096, 1024], P(None, 'head'), may hold values from -0.09375 to 0.09375
- o_weight: bfloat16 [4096, 4096], P('head'), may hold values from -0.5 to 0.5
Outputs:
- mixed: bfloat16 [4096, 4096], P(('groups', 'ctx'), 'head'), parts along dimension 0
The draws below stay inside these ranges and needn't reach their ends.
There are 2 independent parts, one for each index of `groups`. The reference program is written for one: setup_inputs(seed, part) draws one part's arguments, and reference() takes and returns one part's arrays. A program takes and returns all parts, laid end to end along the dimension named above; an argument that names none is the same for every part. Nothing has to cross between parts.
Inputs may be any that keep to these rules, and one draw needn't show every extreme that they name: lengths sum to 2048, and the longest document has exactly 1024 tokens.
All inputs are finite; a program needn't handle non-finite values.
Results may differ from the reference program's by a relative error of at most 0.017.
Values may be sent and summed in bfloat16 or wider, within the bound.
A program may use at most 320 MiB of HBM per device.

```python
import math
import jax
import jax.numpy as jnp
import numpy as np
from jax import lax

D = 4096
HD = 128
KVH = 8
QH = 32
TOK_DEV = 512
TOKENS = 2048
DOC_MOST = 1024
NDOCS = 16
N_CTX = 4
N_HEAD = 4


def draw_tokens(key, part):
    return jnp.clip(jax.random.normal(key, (TOKENS, D), jnp.float32), -6.0, 6.0).astype(jnp.bfloat16)


def draw_q_weight(key, part):
    noise = jnp.clip(jax.random.normal(key, (D, QH * HD), jnp.float32), -6.0, 6.0)
    return (noise * D ** (-0.5)).astype(jnp.bfloat16)


def draw_k_weight(key, part):
    noise = jnp.clip(jax.random.normal(key, (D, KVH * HD), jnp.float32), -6.0, 6.0)
    return (noise * D ** (-0.5)).astype(jnp.bfloat16)


def block_scale(rng, shape, pieces, smallest, top_value):
    def one(position, parts):
        heights = jax.random.uniform(jax.random.fold_in(jax.random.fold_in(rng, 6), position), (parts,), jnp.float32, smallest / len(pieces), top_value / len(pieces))
        return jnp.repeat(jnp.exp(heights), shape[position] // parts).reshape((-1,) + (1,) * (len(shape) - position - 1))

    level = one(*pieces[0])
    for cut in pieces[1:]:
        level = level * one(*cut)
    return level


def split_up(count, total, bound, lean):
    portions = [(1 << 20) // math.isqrt(rank ** lean) + 1 for rank in range(2, count + 1)]
    rest, given = total - bound - (count - 1), [1] * (count - 1)
    while rest > 0:
        movable = [i for i in range(count - 1) if given[i] < bound]
        mass, budget = sum([portions[i] for i in movable]), rest
        for i in movable:
            addition = min(bound - given[i], max(1, budget * portions[i] // mass), rest)
            given[i] = given[i] + addition
            rest = rest - addition
    return np.array([bound] + given)


def uneven_parts(own_key, count, total, reach, lean):
    if count == 2:
        one = jax.random.randint(own_key, (), max(1, total - reach), min(reach, total - 1) + 1)
        return jnp.stack([one, total - one])
    sizes = jnp.asarray(split_up(count, total, reach, lean), jnp.int32)
    couples = (count - 1) // 2
    giver, taker = sizes[1:1 + 2 * couples:2], sizes[2:2 + 2 * couples:2]
    slack = jnp.minimum(giver - 1, reach - taker)
    moved = jax.random.randint(jax.random.fold_in(own_key, 1), (couples,), 0, 1 << 20) % (slack + 1)
    sizes = sizes.at[1:1 + 2 * couples:2].set(giver - moved).at[2:2 + 2 * couples:2].set(taker + moved)
    return sizes[jax.random.permutation(jax.random.fold_in(own_key, 2), count)]


def gaussian(key, extent, deviation, reach, shards=(), held_as=jnp.bfloat16):
    loudness = block_scale(key, extent, shards, -0.22, 0.18) if shards else 1.0
    entries = jax.random.normal(key, extent, jnp.float32) * deviation * loudness
    return jnp.minimum(jnp.maximum(entries, -reach), reach).astype(held_as)


def setup_inputs(seed: int = 0, part: int = 0) -> dict:
    seeds = jax.random.split(jax.random.key(seed), 7)
    part_splits = jax.random.split(jax.random.fold_in(seeds[6], part), 7)
    tokens = draw_tokens(jax.random.fold_in(jax.random.fold_in(seeds[6], part), 71), part)
    lengths = uneven_parts(part_splits[1], NDOCS, TOKENS, DOC_MOST, 2).astype(jnp.int32)
    q_weight = draw_q_weight(jax.random.fold_in(seeds[6], 71), part)
    k_weight = draw_k_weight(jax.random.fold_in(seeds[6], 71), part)
    v_weight = gaussian(seeds[4], (D, KVH * HD), D ** -0.5, 0.09375, ((1, 4),))
    o_weight = gaussian(seeds[5], (QH * HD, D), (QH * HD // 32) ** -0.5, 0.5, ((0, 4),))
    return {"tokens": tokens, "lengths": lengths, "q_weight": q_weight, "k_weight": k_weight, "v_weight": v_weight, "o_weight": o_weight}


def fold_positions(rows, shard_rows, shard_count):
    shard = rows // shard_rows
    inner = rows % shard_rows
    half_rows = shard_rows // 2
    block = jnp.where(inner < half_rows, shard, 2 * shard_count - 1 - shard)
    return (block * half_rows + inner % half_rows).astype(jnp.int32)

def doc_info(place, lengths):
    ends = jnp.cumsum(lengths).astype(jnp.int32)
    passed = ends[None, :] <= place[:, None]
    document = lax.optimization_barrier(jnp.sum(passed.astype(jnp.int32), axis=1)).astype(jnp.int32)
    first = lax.optimization_barrier(jnp.sum(jnp.where(passed, lengths[None, :], 0), axis=1)).astype(jnp.int32)
    return (document, first)

def rotate(values, offset):
    half_size = values.shape[-1] // 2
    expo = jnp.arange(half_size).astype(jnp.float32) * (2.0 / values.shape[-1])
    inverse = jnp.exp(-math.log(500000.0) * expo)
    angle = offset.astype(jnp.float32)[:, None] * inverse[None, :]
    cosine = jnp.cos(angle)[:, None, :]
    sine = jnp.sin(angle)[:, None, :]
    left = values[..., :half_size]
    right = values[..., half_size:]
    return jnp.concatenate([left * cosine - right * sine, right * cosine + left * sine], axis=-1)

def rms_norm(tokens):
    wide = tokens.astype(jnp.float32)
    scale = lax.rsqrt(lax.optimization_barrier(jnp.mean(wide * wide, axis=-1, keepdims=True)) + 1e-05)
    return (wide * scale).astype(jnp.bfloat16)

def reference(tokens, lengths, q_weight, k_weight, v_weight, o_weight):
    count = tokens.shape[0]
    rows = jnp.arange(count, dtype=jnp.int32)
    place = fold_positions(rows, TOK_DEV, N_CTX)
    document, first = doc_info(place, lengths)
    offset = place - first
    normed = rms_norm(tokens)
    group = QH // KVH
    query = rotate(jnp.dot(normed, q_weight, preferred_element_type=jnp.float32).reshape(count, QH, HD), offset).astype(jnp.bfloat16)
    query = query.reshape(count, KVH, group, HD)
    keys = rotate(jnp.dot(normed, k_weight, preferred_element_type=jnp.float32).reshape(count, KVH, HD), offset).astype(jnp.bfloat16)
    values = jnp.dot(normed, v_weight, preferred_element_type=jnp.float32).astype(jnp.bfloat16).reshape(count, KVH, HD)
    keys_wide = keys.astype(jnp.float32)
    values_wide = values.astype(jnp.float32)
    block_rows = math.gcd(count, 512)
    blocks = count // block_rows

    def one_block(index):
        begin = (index * block_rows).astype(jnp.int32)
        query_block = lax.dynamic_slice_in_dim(query, begin, block_rows, 0).astype(jnp.float32)
        place_block = lax.dynamic_slice_in_dim(place, begin, block_rows, 0)
        doc_block = lax.dynamic_slice_in_dim(document, begin, block_rows, 0)
        scores = jnp.einsum('tkgd,skd->kgts', query_block, keys_wide) * (1.0 / math.sqrt(HD))
        allowed = (document[None, :] == doc_block[:, None]) & (place[None, :] <= place_block[:, None])
        scores = jnp.where(allowed, scores, -1e+30)
        top = lax.optimization_barrier(jnp.max(scores, axis=-1, keepdims=True))
        expo = jnp.where(allowed, jnp.exp(scores - top), 0.0)
        total = lax.optimization_barrier(jnp.sum(expo, axis=-1))
        weights = expo.astype(jnp.bfloat16).astype(jnp.float32)
        summed = jnp.einsum('kgts,skd->kgtd', weights, values_wide)
        result = (summed / total[..., None]).astype(jnp.bfloat16)
        return jnp.transpose(result, (2, 0, 1, 3)).reshape(block_rows, QH * HD)
    attended = lax.map(one_block, jnp.arange(blocks, dtype=jnp.int32)).reshape(count, QH * HD)
    width = QH * HD // N_HEAD
    mixed = jnp.zeros((count, D), jnp.float32)
    for index in range(N_HEAD):
        partial_value = jnp.dot(attended[:, index * width:(index + 1) * width], o_weight[index * width:(index + 1) * width], preferred_element_type=jnp.float32)
        rounded = lax.optimization_barrier(partial_value.astype(jnp.bfloat16))
        mixed = mixed + rounded.astype(jnp.float32)
    return mixed.astype(jnp.bfloat16)
```

```python
import functools
import math

import jax
import jax.numpy as jnp
from jax import lax
from jax.experimental import pallas as pl
from jax.experimental.pallas import tpu as pltpu
from jax.sharding import PartitionSpec as P

HD = 128
MESH = pl.DeviceIdType.MESH
LOW = -1e30


def tables(lengths, rows, ctx_count):
    half = rows // 2
    device = lax.axis_index("ctx")
    inner = jnp.arange(rows, dtype=jnp.int32)
    block = jnp.where(inner < half, device, 2 * ctx_count - 1 - device)
    place = block * half + inner % half
    ends = jnp.cumsum(lengths)
    passed = ends[None, :] <= place[:, None]
    first = jnp.sum(jnp.where(passed, lengths[None, :], 0), axis=1)
    offset = (place - first).astype(jnp.float32)
    expo = jnp.arange(HD // 2).astype(jnp.float32) * (2.0 / HD)
    inverse = jnp.exp(-math.log(500000.0) * expo)
    angle = offset[:, None] * inverse[None, :]
    cosine, sine = jnp.cos(angle), jnp.sin(angle)
    return (
        first.astype(jnp.int32)[None, :],
        jnp.concatenate([cosine, cosine], axis=1),
        jnp.concatenate([-sine, sine], axis=1),
    )


def rotated(values, cosine, sine):
    return values * cosine + pltpu.roll(values, HD // 2, 1) * sine


def kernel(
    n, n_head, first_ref, cos_ref, sin_ref, tok_hbm, qw_hbm, kw_hbm, vw_hbm, ow_hbm,
    out_ref,
    tok, qw, kvw, ow, kv_acc, norm, query, keys, values, top, total, accum, attended,
    own, kept, sib_out, sib_in, far_out, far_in,
    tok_sem, kw_sem, vw_sem, qw_sem, ow_sem,
    kv_send, kv_recv, sib_send, sib_recv, far_send, far_recv,
):
    rows, depth = tok.shape
    half = rows // 2
    kv_heads = keys.shape[1]
    q_heads = query.shape[0]
    group = q_heads // kv_heads
    k_cols = kv_heads * HD
    chips = n_head // 2
    width = out_ref.shape[1]
    pieces = 4
    piece = depth // pieces

    c = lax.axis_index("ctx")
    head = lax.axis_index("head")
    chip, core = lax.div(head, 2), lax.rem(head, 2)
    sibling = chip * 2 + 1 - core
    has_left, has_right = c > 0, c < n - 1
    low_block, high_block = c, 2 * n - 1 - c

    def other_chip(step):
        return lax.rem(chip + step, chips)

    def load_piece(k):
        cols = pl.ds(pl.multiple_of(k * piece, piece), piece)
        return (
            pltpu.make_async_copy(tok_hbm.at[:, cols], tok.at[:, cols], tok_sem.at[k]),
            pltpu.make_async_copy(kw_hbm.at[cols, :], kvw.at[cols, 0:k_cols], kw_sem.at[k]),
            pltpu.make_async_copy(
                vw_hbm.at[cols, :], kvw.at[cols, k_cols : 2 * k_cols], vw_sem.at[k]
            ),
        )

    for k in range(pieces):
        for copy in load_piece(k):
            copy.start()
    load_q = pltpu.make_async_copy(qw_hbm, qw, qw_sem)
    load_o = pltpu.make_async_copy(ow_hbm, ow, ow_sem)

    barrier = pltpu.get_barrier_semaphore()

    def greet(target):
        pl.semaphore_signal(barrier, inc=1, device_id=target, device_id_type=MESH)

    @pl.when(has_left)
    def _():
        greet({"ctx": c - 1})

    @pl.when(has_right)
    def _():
        greet({"ctx": c + 1})

    greet({"head": sibling})
    for step in range(1, chips):
        greet({"head": other_chip(step) * 2 + core})

    kv_acc[...] = jnp.zeros_like(kv_acc)
    norm[...] = jnp.zeros_like(norm)

    def project_piece(k, carry):
        for copy in load_piece(k):
            copy.wait()
        cols = pl.ds(pl.multiple_of(k * piece, piece), piece)

        def squares(r, inner):
            at = pl.ds(pl.multiple_of(r * 64, 64), 64)
            wide = tok[at, cols].astype(jnp.float32)
            sq = wide * wide
            part = sq[:, 0:HD]
            for s in range(1, piece // HD):
                part = part + sq[:, s * HD : (s + 1) * HD]
            norm[at, :] += part
            return inner

        lax.fori_loop(0, rows // 64, squares, 0)
        kv_acc[...] += jnp.dot(tok[:, cols], kvw[cols, :], preferred_element_type=jnp.float32)
        return carry

    lax.fori_loop(0, pieces, project_piece, 0)
    load_q.start()
    load_o.start()
    mean = jnp.sum(norm[...], axis=1, keepdims=True) * (1.0 / depth)
    norm[...] = jnp.broadcast_to(lax.rsqrt(mean + 1e-05), norm.shape)
    for g in range(kv_heads):
        for side, block in ((0, low_block), (1, high_block)):
            at = slice(side * half, (side + 1) * half)
            raw = kv_acc[at, g * HD : (g + 1) * HD] * norm[at, :]
            keys[block, g] = rotated(raw, cos_ref[at, :], sin_ref[at, :]).astype(jnp.bfloat16)
            raw = kv_acc[at, k_cols + g * HD : k_cols + (g + 1) * HD] * norm[at, :]
            values[block, g] = raw.T.astype(jnp.bfloat16)

    def block_copies(block, way):
        target = {"ctx": c + 1 if way else c - 1}
        return [
            pltpu.make_async_remote_copy(
                src_ref=ref.at[block],
                dst_ref=ref.at[block],
                send_sem=kv_send.at[way, kind, block],
                recv_sem=kv_recv.at[kind, block],
                device_id=target,
                device_id_type=MESH,
            )
            for kind, ref in enumerate((keys, values))
        ]

    def send(block, way):
        for copy in block_copies(block, way):
            copy.start()

    def receive(block):
        for copy in block_copies(block, 0):
            copy.wait_recv()

    greeted = 1 + (chips - 1) + has_left.astype(jnp.int32) + has_right.astype(jnp.int32)
    pl.semaphore_wait(barrier, greeted)

    @pl.when(has_right)
    def _():
        send(low_block, 1)

    @pl.when(has_left)
    def _():
        send(high_block, 0)

    load_q.wait()
    factor = math.log2(math.e) / math.sqrt(HD)
    tile = min(256, q_heads * HD)

    def project_query(t, carry):
        cols = pl.ds(pl.multiple_of(t * tile, tile), tile)
        raw = jnp.dot(tok[...], qw[:, cols], preferred_element_type=jnp.float32)
        for h in range(tile // HD):
            part = raw[:, h * HD : (h + 1) * HD] * (norm[...] * factor)
            query[t * (tile // HD) + h] = rotated(part, cos_ref[...], sin_ref[...]).astype(
                jnp.bfloat16
            )
        return carry

    lax.fori_loop(0, q_heads * HD // tile, project_query, 0)

    def attend(side, block, diagonal):
        at = pl.ds(pl.multiple_of(side * half, half), half)

        def one_group(g, carry):
            k = keys[block, g]
            v = values[block, g]
            key_at = lax.broadcasted_iota(jnp.int32, (half, half), 0)
            allowed = key_at >= first_ref[:, at] - block * half
            if diagonal:
                allowed = allowed & (key_at <= lax.broadcasted_iota(jnp.int32, (half, half), 1))
            for j in range(group):
                h = g * group + j
                slot = side * q_heads + h
                scores = lax.dot_general(
                    k, query[h, at, :], (((1,), (1,)), ((), ())),
                    preferred_element_type=jnp.float32,
                )
                scores = jnp.where(allowed, scores, LOW)
                here = jnp.max(scores, axis=0, keepdims=True)
                if not diagonal:
                    before = top[slot]
                    here = jnp.maximum(before, here)
                expo = jnp.exp2(scores - here)
                summed = jnp.sum(expo, axis=0, keepdims=True)
                fresh = jnp.dot(v, expo.astype(jnp.bfloat16), preferred_element_type=jnp.float32)
                if not diagonal:
                    shrink = jnp.exp2(before - here)
                    summed = summed + total[slot] * shrink
                    fresh = fresh + accum[slot] * shrink
                top[slot] = here
                total[slot] = summed
                accum[slot] = fresh
            return carry

        lax.fori_loop(0, kv_heads, one_group, 0)

    def sib_copy(side, x):
        return pltpu.make_async_remote_copy(
            src_ref=sib_out.at[side, x],
            dst_ref=sib_in.at[side, x],
            send_sem=sib_send.at[side, x],
            recv_sem=sib_recv.at[side, x],
            device_id={"head": sibling},
            device_id_type=MESH,
        )

    def far_copy(side, step):
        x = other_chip(step)
        return pltpu.make_async_remote_copy(
            src_ref=far_out.at[side, step - 1],
            dst_ref=far_in.at[side, step - 1],
            send_sem=far_send.at[side, step - 1],
            recv_sem=far_recv.at[side, step - 1],
            device_id={"head": x * 2 + core},
            device_id_type=MESH,
        )

    out_tile = min(256, width)

    def project_out(owner, store):
        def one_tile(t, carry):
            start = pl.multiple_of(owner * width + t * out_tile, out_tile)
            part = jnp.dot(
                attended[...], ow[:, pl.ds(start, out_tile)], preferred_element_type=jnp.float32
            )
            store(pl.ds(pl.multiple_of(t * out_tile, out_tile), out_tile), part)
            return carry

        lax.fori_loop(0, width // out_tile, one_tile, 0)

    def finish(side):
        for h in range(q_heads):
            slot = side * q_heads + h
            result = accum[slot] / total[slot]
            attended[:, h * HD : (h + 1) * HD] = result.T.astype(jnp.bfloat16)
        for step in list(range(1, chips)) + [0]:
            x = other_chip(step)

            def to_sibling(at, part):
                sib_out[side, x, :, at] = part.astype(jnp.bfloat16)

            project_out(x * 2 + 1 - core, to_sibling)
            sib_copy(side, x).start()
        for step in range(1, chips):
            x = other_chip(step)

            def to_own(at, part):
                own[:, at] = part

            project_out(x * 2 + core, to_own)
            sib_copy(side, x).wait_recv()
            far_out[side, step - 1] = (
                own[...] + sib_in[side, x].astype(jnp.float32)
            ).astype(jnp.bfloat16)
            far_copy(side, step).start()

        def to_kept(at, part):
            kept[side, :, at] = part

        project_out(chip * 2 + core, to_kept)

    attend(0, low_block, True)
    attend(1, high_block, True)

    @pl.when(c >= n - 1 - c)
    def _():
        attend(1, low_block, False)

    load_o.wait()
    last_right = jnp.maximum(c + 1, n - 1 - c)
    right_count = jnp.where(has_right, 2 * n - 1 - c - last_right, 0)

    def turn(i, carry):
        left_block, right_block = c - i, 2 * n - 1 - c - i
        from_left = (i >= 1) & (i <= c)
        from_right = (i >= 1) & (i <= right_count)

        @pl.when(from_left)
        def _():
            receive(left_block)

            @pl.when(has_right)
            def _():
                send(left_block, 1)

        @pl.when(from_right)
        def _():
            receive(right_block)

            @pl.when(has_left & (right_block >= n - c))
            def _():
                send(right_block, 0)

        @pl.when((i == right_count) & has_left & (c >= n - c))
        def _():
            send(low_block, 0)

        @pl.when(from_left)
        def _():
            attend(0, left_block, False)

        @pl.when(i == c)
        def _():
            finish(0)

        @pl.when(from_left & (left_block >= n - 1 - c))
        def _():
            attend(1, left_block, False)

        @pl.when(from_right)
        def _():
            attend(1, right_block, False)

        return carry

    lax.fori_loop(0, n + 1, turn, 0)
    finish(1)

    for side in range(2):
        sib_copy(side, chip).wait_recv()
        mixed = kept[side] + sib_in[side, chip].astype(jnp.float32)
        for step in range(1, chips):
            far_copy(side, step).wait_recv()
            mixed = mixed + far_in[side, step - 1].astype(jnp.float32)
        out_ref[side * half : (side + 1) * half, :] = mixed.astype(jnp.bfloat16)

    for side in range(2):
        for x in range(chips):
            sib_copy(side, x).wait_send()
        for step in range(1, chips):
            far_copy(side, step).wait_send()

    def drain(block, carry):
        @pl.when(has_right & (block <= c))
        def _():
            for copy in block_copies(block, 1):
                copy.wait_send()

        @pl.when(has_left & (block >= jnp.maximum(c, n - c)) & (block <= high_block))
        def _():
            for copy in block_copies(block, 0):
                copy.wait_send()

        return carry

    lax.fori_loop(0, 2 * n, drain, 0)


def shards(n, n_head, tokens, lengths, q_weight, k_weight, v_weight, o_weight):
    rows, depth = tokens.shape
    half = rows // 2
    q_cols, k_cols = q_weight.shape[1], k_weight.shape[1]
    q_heads, kv_heads = q_cols // HD, k_cols // HD
    chips = n_head // 2
    width = o_weight.shape[1] // n_head
    first, cosine, sine = tables(lengths, rows, n)
    bf16, f32 = jnp.bfloat16, jnp.float32
    dma = pltpu.SemaphoreType.DMA
    far = max(chips - 1, 1)
    vmem = pl.BlockSpec(memory_space=pltpu.VMEM)
    hbm = pl.BlockSpec(memory_space=pl.ANY)
    return pl.pallas_call(
        functools.partial(kernel, n, n_head),
        out_shape=jax.ShapeDtypeStruct((rows, width), bf16),
        in_specs=[vmem] * 3 + [hbm] * 5,
        out_specs=vmem,
        scratch_shapes=[
            pltpu.VMEM((rows, depth), bf16),
            pltpu.VMEM((depth, q_cols), bf16),
            pltpu.VMEM((depth, 2 * k_cols), bf16),
            pltpu.VMEM(o_weight.shape, bf16),
            pltpu.VMEM((rows, 2 * k_cols), f32),
            pltpu.VMEM((rows, HD), f32),
            pltpu.VMEM((q_heads, rows, HD), bf16),
            pltpu.VMEM((2 * n, kv_heads, half, HD), bf16),
            pltpu.VMEM((2 * n, kv_heads, HD, half), bf16),
            pltpu.VMEM((2 * q_heads, 1, half), f32),
            pltpu.VMEM((2 * q_heads, 1, half), f32),
            pltpu.VMEM((2 * q_heads, HD, half), f32),
            pltpu.VMEM((half, q_cols), bf16),
            pltpu.VMEM((half, width), f32),
            pltpu.VMEM((2, half, width), f32),
            pltpu.VMEM((2, chips, half, width), bf16),
            pltpu.VMEM((2, chips, half, width), bf16),
            pltpu.VMEM((2, far, half, width), bf16),
            pltpu.VMEM((2, far, half, width), bf16),
            dma((4,)), dma((4,)), dma((4,)), dma, dma,
            dma((2, 2, 2 * n)), dma((2, 2 * n)),
            dma((2, chips)), dma((2, chips)),
            dma((2, far)), dma((2, far)),
        ],
        compiler_params=pltpu.CompilerParams(
            collective_id=0, has_side_effects=True, vmem_limit_bytes=60 * 2**20
        ),
    )(first, cosine, sine, tokens, q_weight, k_weight, v_weight, o_weight)


def solution(mesh):
    return jax.shard_map(
        functools.partial(shards, mesh.shape["ctx"], mesh.shape["head"]),
        mesh=mesh,
        in_specs=(
            P(("groups", "ctx"), None),
            P("groups"),
            P(None, "head"),
            P(None, "head"),
            P(None, "head"),
            P("head", None),
        ),
        out_specs=P(("groups", "ctx"), "head"),
        check_vma=False,
    )
```

```python
import functools
import math

import jax
import jax.numpy as jnp
from jax import lax
from jax.experimental import pallas as pl
from jax.experimental.pallas import tpu as pltpu
from jax.sharding import PartitionSpec as P

HD = 128
MESH = pl.DeviceIdType.MESH
LOW = -1e30


def rotated(values, cosine, sine):
    return values * cosine + pltpu.roll(values, HD // 2, 1) * sine


def kernel(
    n, n_head, lengths_ref, tok_hbm, qw_hbm, kw_hbm, vw_hbm, ow_hbm,
    out_ref,
    first_ref, cos_ref, sin_ref, tok, qw, kvw, ow, kv_acc, norm, query, keys, values, top, total, accum, attended,
    own, kept, sib_out, sib_in, far_out, far_in,
    tok_sem, kw_sem, vw_sem, qw_sem, ow_sem,
    kv_send, kv_recv, sib_send, sib_recv, far_send, far_recv,
):
    rows, depth = tok.shape
    half = rows // 2
    kv_heads = keys.shape[1]
    group = query.shape[2] // half
    q_heads = kv_heads * group
    wide_rows = group * half
    k_cols = kv_heads * HD
    chips = n_head // 2
    width = out_ref.shape[1]
    pieces = 4
    piece = depth // pieces

    c = lax.axis_index("ctx")
    head = lax.axis_index("head")
    chip, core = lax.div(head, 2), lax.rem(head, 2)
    sibling = chip * 2 + 1 - core
    has_left, has_right = c > 0, c < n - 1
    low_block, high_block = c, 2 * n - 1 - c

    def other_chip(step):
        return lax.rem(chip + step, chips)

    def load_piece(k):
        cols = pl.ds(pl.multiple_of(k * piece, piece), piece)
        return (
            pltpu.make_async_copy(tok_hbm.at[:, cols], tok.at[:, cols], tok_sem.at[k]),
            pltpu.make_async_copy(kw_hbm.at[cols, :], kvw.at[cols, 0:k_cols], kw_sem.at[k]),
            pltpu.make_async_copy(
                vw_hbm.at[cols, :], kvw.at[cols, k_cols : 2 * k_cols], vw_sem.at[k]
            ),
        )

    for k in range(pieces):
        for copy in load_piece(k):
            copy.start()
    load_q = pltpu.make_async_copy(qw_hbm, qw, qw_sem)
    load_o = pltpu.make_async_copy(ow_hbm, ow, ow_sem)

    barrier = pltpu.get_barrier_semaphore()

    def greet(target):
        pl.semaphore_signal(barrier, inc=1, device_id=target, device_id_type=MESH)

    @pl.when(has_left)
    def _():
        greet({"ctx": c - 1})

    @pl.when(has_right)
    def _():
        greet({"ctx": c + 1})

    greet({"head": sibling})
    for step in range(1, chips):
        greet({"head": other_chip(step) * 2 + core})

    def starts(place):
        first, end = jnp.zeros_like(place), 0
        for d in range(lengths_ref.shape[0]):
            end = end + lengths_ref[d]
            first = jnp.where(place >= end, end, first)
        return first

    for side, block in ((0, low_block), (1, high_block)):
        lane = lax.broadcasted_iota(jnp.int32, (1, half), 1)
        row_first = starts(block * half + lane)
        first_ref[side] = jnp.concatenate([row_first] * group, axis=1)
    lane = lax.broadcasted_iota(jnp.int32, (half, HD), 1)
    on_left = lane < HD // 2
    place = jnp.where(on_left, low_block, high_block) * half + lax.broadcasted_iota(
        jnp.int32, (half, HD), 0
    )
    offset = (place - starts(place)).astype(jnp.float32)
    expo = (lane % (HD // 2)).astype(jnp.float32) * (2.0 / HD)
    angle = offset * jnp.exp(-math.log(500000.0) * expo)
    cosine, sine = jnp.cos(angle), jnp.sin(angle)
    cosine_over, sine_over = pltpu.roll(cosine, HD // 2, 1), pltpu.roll(sine, HD // 2, 1)
    cos_ref[0:half, :] = jnp.where(on_left, cosine, cosine_over)
    cos_ref[half:rows, :] = jnp.where(on_left, cosine_over, cosine)
    sin_ref[0:half, :] = jnp.where(on_left, -sine, sine_over)
    sin_ref[half:rows, :] = jnp.where(on_left, -sine_over, sine)

    kv_acc[...] = jnp.zeros_like(kv_acc)
    norm[...] = jnp.zeros_like(norm)

    def project_piece(k, carry):
        for copy in load_piece(k):
            copy.wait()
        cols = pl.ds(pl.multiple_of(k * piece, piece), piece)

        def squares(r, inner):
            at = pl.ds(pl.multiple_of(r * 64, 64), 64)
            wide = tok[at, cols].astype(jnp.float32)
            sq = wide * wide
            part = sq[:, 0:HD]
            for s in range(1, piece // HD):
                part = part + sq[:, s * HD : (s + 1) * HD]
            norm[at, :] += part
            return inner

        lax.fori_loop(0, rows // 64, squares, 0)
        kv_acc[...] += jnp.dot(tok[:, cols], kvw[cols, :], preferred_element_type=jnp.float32)
        return carry

    lax.fori_loop(0, pieces, project_piece, 0)
    load_q.start()
    load_o.start()
    mean = jnp.sum(norm[...], axis=1, keepdims=True) * (1.0 / depth)
    norm[...] = jnp.broadcast_to(lax.rsqrt(mean + 1e-05), norm.shape)
    for g in range(kv_heads):
        for side, block in ((0, low_block), (1, high_block)):
            at = slice(side * half, (side + 1) * half)
            raw = kv_acc[at, g * HD : (g + 1) * HD] * norm[at, :]
            keys[block, g] = rotated(raw, cos_ref[at, :], sin_ref[at, :]).astype(jnp.bfloat16)
            raw = kv_acc[at, k_cols + g * HD : k_cols + (g + 1) * HD] * norm[at, :]
            values[block, g] = raw.T.astype(jnp.bfloat16)

    def block_copies(block, way):
        target = {"ctx": c + 1 if way else c - 1}
        return [
            pltpu.make_async_remote_copy(
                src_ref=ref.at[block],
                dst_ref=ref.at[block],
                send_sem=kv_send.at[way, kind, block],
                recv_sem=kv_recv.at[kind, block],
                device_id=target,
                device_id_type=MESH,
            )
            for kind, ref in enumerate((keys, values))
        ]

    def send(block, way):
        for copy in block_copies(block, way):
            copy.start()

    def receive(block):
        for copy in block_copies(block, 0):
            copy.wait_recv()

    greeted = 1 + (chips - 1) + has_left.astype(jnp.int32) + has_right.astype(jnp.int32)
    pl.semaphore_wait(barrier, greeted)

    @pl.when(has_right)
    def _():
        send(low_block, 1)

    @pl.when(has_left)
    def _():
        send(high_block, 0)

    load_q.wait()
    factor = math.log2(math.e) / math.sqrt(HD)
    tile = min(256, q_heads * HD)

    def project_query(t, carry):
        cols = pl.ds(pl.multiple_of(t * tile, tile), tile)
        raw = jnp.dot(tok[...], qw[:, cols], preferred_element_type=jnp.float32)
        for h in range(tile // HD):
            part = raw[:, h * HD : (h + 1) * HD] * (norm[...] * factor)
            turned = rotated(part, cos_ref[...], sin_ref[...]).astype(jnp.bfloat16)
            at_head = t * (tile // HD) + h
            g, j = lax.div(at_head, group), lax.rem(at_head, group)
            at = pl.ds(pl.multiple_of(j * half, half), half)
            for side in range(2):
                query[g, side, at, :] = turned[side * half : (side + 1) * half]
        return carry

    lax.fori_loop(0, q_heads * HD // tile, project_query, 0)

    def attend(side, block, diagonal):
        def one_group(g, carry):
            slot = side * kv_heads + g
            key_at = lax.broadcasted_iota(jnp.int32, (half, wide_rows), 0)
            allowed = key_at >= first_ref[side] - block * half
            if diagonal:
                row_at = lax.broadcasted_iota(jnp.int32, (1, wide_rows), 1) % half
                allowed = allowed & (key_at <= row_at)
            scores = lax.dot_general(
                keys[block, g], query[g, side], (((1,), (1,)), ((), ())),
                preferred_element_type=jnp.float32,
            )
            scores = jnp.where(allowed, scores, LOW)
            here = jnp.max(scores, axis=0, keepdims=True)
            if not diagonal:
                before = top[slot]
                here = jnp.maximum(before, here)
            expo = jnp.exp2(scores - here)
            summed = jnp.sum(expo, axis=0, keepdims=True)
            fresh = jnp.dot(
                values[block, g], expo.astype(jnp.bfloat16), preferred_element_type=jnp.float32
            )
            if not diagonal:
                shrink = jnp.exp2(before - here)
                summed = summed + total[slot] * shrink
                fresh = fresh + accum[slot] * shrink
            top[slot] = here
            total[slot] = summed
            accum[slot] = fresh
            return carry

        lax.fori_loop(0, kv_heads, one_group, 0)

    def sib_copy(side, x):
        return pltpu.make_async_remote_copy(
            src_ref=sib_out.at[side, x],
            dst_ref=sib_in.at[side, x],
            send_sem=sib_send.at[side, x],
            recv_sem=sib_recv.at[side, x],
            device_id={"head": sibling},
            device_id_type=MESH,
        )

    def far_copy(side, step):
        x = other_chip(step)
        return pltpu.make_async_remote_copy(
            src_ref=far_out.at[side, step - 1],
            dst_ref=far_in.at[side, step - 1],
            send_sem=far_send.at[side, step - 1],
            recv_sem=far_recv.at[side, step - 1],
            device_id={"head": x * 2 + core},
            device_id_type=MESH,
        )

    out_tile = min(256, width)

    def project_out(owner, store):
        def one_tile(t, carry):
            start = pl.multiple_of(owner * width + t * out_tile, out_tile)
            part = jnp.dot(
                attended[...], ow[:, pl.ds(start, out_tile)], preferred_element_type=jnp.float32
            )
            store(pl.ds(pl.multiple_of(t * out_tile, out_tile), out_tile), part)
            return carry

        lax.fori_loop(0, width // out_tile, one_tile, 0)

    def finish(side):
        for g in range(kv_heads):
            slot = side * kv_heads + g
            result = accum[slot] * (1.0 / total[slot])
            for j in range(group):
                h = g * group + j
                part = result[:, j * half : (j + 1) * half]
                attended[:, h * HD : (h + 1) * HD] = part.T.astype(jnp.bfloat16)
        for step in list(range(1, chips)) + [0]:
            x = other_chip(step)

            def to_sibling(at, part):
                sib_out[side, x, :, at] = part.astype(jnp.bfloat16)

            def to_own(at, part):
                if step:
                    own[:, at] = part
                else:
                    kept[side, :, at] = part

            project_out(x * 2 + 1 - core, to_sibling)
            sib_copy(side, x).start()
            project_out(x * 2 + core, to_own)
            if step:
                sib_copy(side, x).wait_recv()
                far_out[side, step - 1] = (
                    own[...] + sib_in[side, x].astype(jnp.float32)
                ).astype(jnp.bfloat16)
                far_copy(side, step).start()

    load_o.wait()
    last_right = jnp.maximum(c + 1, n - 1 - c)
    right_count = jnp.where(has_right, 2 * n - 1 - c - last_right, 0)

    def from_left(i):
        return (i >= 1) & (i <= c)

    def from_right(i):
        return (i >= 1) & (i <= right_count)

    def passes_right(i):
        return from_left(i) & has_right

    def passes_left(i):
        return from_right(i) & has_left & (2 * n - 1 - c - i >= n - c)

    def arrive(i):
        @pl.when(from_left(i))
        def _():
            receive(c - i)

            @pl.when(has_right)
            def _():
                send(c - i, 1)

        @pl.when(from_right(i))
        def _():
            receive(2 * n - 1 - c - i)

            @pl.when(passes_left(i))
            def _():
                send(2 * n - 1 - c - i, 0)

        @pl.when((i == right_count) & has_left & (c >= n - c))
        def _():
            send(low_block, 0)

    arrive(0)

    def turn(i, carry):
        early = passes_right(i + 1) | passes_left(i + 1)

        @pl.when(early)
        def _():
            arrive(i + 1)

        @pl.when(i == 0)
        def _():
            attend(0, low_block, True)
            attend(1, high_block, True)

        @pl.when(from_left(i))
        def _():
            attend(0, c - i, False)

        @pl.when(i == c)
        def _():
            finish(0)

        @pl.when((i <= c) & (c - i >= n - 1 - c))
        def _():
            attend(1, c - i, False)

        @pl.when(from_right(i))
        def _():
            attend(1, 2 * n - 1 - c - i, False)

        @pl.when(jnp.logical_not(early))
        def _():
            arrive(i + 1)

        return carry

    lax.fori_loop(0, n + 1, turn, 0)
    finish(1)

    for side in range(2):
        sib_copy(side, chip).wait_recv()
        mixed = kept[side] + sib_in[side, chip].astype(jnp.float32)
        for step in range(1, chips):
            far_copy(side, step).wait_recv()
            mixed = mixed + far_in[side, step - 1].astype(jnp.float32)
        out_ref[side * half : (side + 1) * half, :] = mixed.astype(jnp.bfloat16)

    for side in range(2):
        for x in range(chips):
            sib_copy(side, x).wait_send()
        for step in range(1, chips):
            far_copy(side, step).wait_send()

    def drain(block, carry):
        @pl.when(has_right & (block <= c))
        def _():
            for copy in block_copies(block, 1):
                copy.wait_send()

        @pl.when(has_left & (block >= jnp.maximum(c, n - c)) & (block <= high_block))
        def _():
            for copy in block_copies(block, 0):
                copy.wait_send()

        return carry

    lax.fori_loop(0, 2 * n, drain, 0)


def shards(n, n_head, tokens, lengths, q_weight, k_weight, v_weight, o_weight):
    rows, depth = tokens.shape
    half = rows // 2
    q_cols, k_cols = q_weight.shape[1], k_weight.shape[1]
    q_heads, kv_heads = q_cols // HD, k_cols // HD
    chips = n_head // 2
    width = o_weight.shape[1] // n_head
    group = q_heads // kv_heads
    bf16, f32 = jnp.bfloat16, jnp.float32
    dma = pltpu.SemaphoreType.DMA
    far = max(chips - 1, 1)
    vmem = pl.BlockSpec(memory_space=pltpu.VMEM)
    hbm = pl.BlockSpec(memory_space=pl.ANY)
    return pl.pallas_call(
        functools.partial(kernel, n, n_head),
        out_shape=jax.ShapeDtypeStruct((rows, width), bf16),
        in_specs=[pl.BlockSpec(memory_space=pltpu.SMEM)] + [hbm] * 5,
        out_specs=vmem,
        scratch_shapes=[
            pltpu.VMEM((2, 1, group * half), jnp.int32),
            pltpu.VMEM((rows, HD), f32),
            pltpu.VMEM((rows, HD), f32),
            pltpu.VMEM((rows, depth), bf16),
            pltpu.VMEM((depth, q_cols), bf16),
            pltpu.VMEM((depth, 2 * k_cols), bf16),
            pltpu.VMEM(o_weight.shape, bf16),
            pltpu.VMEM((rows, 2 * k_cols), f32),
            pltpu.VMEM((rows, HD), f32),
            pltpu.VMEM((kv_heads, 2, group * half, HD), bf16),
            pltpu.VMEM((2 * n, kv_heads, half, HD), bf16),
            pltpu.VMEM((2 * n, kv_heads, HD, half), bf16),
            pltpu.VMEM((2 * kv_heads, 1, group * half), f32),
            pltpu.VMEM((2 * kv_heads, 1, group * half), f32),
            pltpu.VMEM((2 * kv_heads, HD, group * half), f32),
            pltpu.VMEM((half, q_cols), bf16),
            pltpu.VMEM((half, width), f32),
            pltpu.VMEM((2, half, width), f32),
            pltpu.VMEM((2, chips, half, width), bf16),
            pltpu.VMEM((2, chips, half, width), bf16),
            pltpu.VMEM((2, far, half, width), bf16),
            pltpu.VMEM((2, far, half, width), bf16),
            dma((4,)), dma((4,)), dma((4,)), dma, dma,
            dma((2, 2, 2 * n)), dma((2, 2 * n)),
            dma((2, chips)), dma((2, chips)),
            dma((2, far)), dma((2, far)),
        ],
        compiler_params=pltpu.CompilerParams(
            collective_id=0, has_side_effects=True, vmem_limit_bytes=60 * 2**20
        ),
    )(lengths, tokens, q_weight, k_weight, v_weight, o_weight)


def solution(mesh):
    return jax.shard_map(
        functools.partial(shards, mesh.shape["ctx"], mesh.shape["head"]),
        mesh=mesh,
        in_specs=(
            P(("groups", "ctx"), None),
            P("groups"),
            P(None, "head"),
            P(None, "head"),
            P(None, "head"),
            P("head", None),
        ),
        out_specs=P(("groups", "ctx"), "head"),
        check_vma=False,
    )
```

```python
import functools
import math

import jax
import jax.numpy as jnp
from jax import lax
from jax.experimental import pallas as pl
from jax.experimental.pallas import tpu as pltpu
from jax.sharding import PartitionSpec as P

HD = 128
MESH = pl.DeviceIdType.MESH
LOW = -1e30


def rotated(values, cosine, sine):
    return values * cosine + pltpu.roll(values, HD // 2, 1) * sine


def kernel(
    n, n_head, lengths_ref, tok_hbm, qw_hbm, kw_hbm, vw_hbm, ow_hbm,
    out_ref,
    first_ref, cos_ref, sin_ref, tok, qw, kvw, ow, kv_acc, norm, query, keys, values, top, total, accum, attended,
    kept, mixed, sib_out, sib_in, far_out, far_in,
    tok_sem, kw_sem, vw_sem, qw_sem, ow_sem,
    kv_send, kv_recv, sib_send, sib_recv, far_send, far_recv, out_sem,
):
    rows, depth = tok.shape
    half = rows // 2
    kv_heads = keys.shape[1]
    group = query.shape[2] // half
    q_heads = kv_heads * group
    wide_rows = group * half
    k_cols = kv_heads * HD
    chips = n_head // 2
    width = out_ref.shape[1]
    pieces = 4
    piece = depth // pieces

    c = lax.axis_index("ctx")
    head = lax.axis_index("head")
    chip, core = lax.div(head, 2), lax.rem(head, 2)
    sibling = chip * 2 + 1 - core
    has_left, has_right = c > 0, c < n - 1
    low_block, high_block = c, 2 * n - 1 - c

    def other_chip(step):
        return lax.rem(chip + step, chips)

    def load_piece(k):
        cols = pl.ds(pl.multiple_of(k * piece, piece), piece)
        return (
            pltpu.make_async_copy(tok_hbm.at[:, cols], tok.at[:, cols], tok_sem.at[k]),
            pltpu.make_async_copy(kw_hbm.at[cols, :], kvw.at[cols, 0:k_cols], kw_sem.at[k]),
            pltpu.make_async_copy(
                vw_hbm.at[cols, :], kvw.at[cols, k_cols : 2 * k_cols], vw_sem.at[k]
            ),
        )

    for k in range(pieces):
        for copy in load_piece(k):
            copy.start()
    load_q = pltpu.make_async_copy(qw_hbm, qw, qw_sem)
    load_o = pltpu.make_async_copy(ow_hbm, ow, ow_sem)

    barrier = pltpu.get_barrier_semaphore()

    def greet(target):
        pl.semaphore_signal(barrier, inc=1, device_id=target, device_id_type=MESH)

    @pl.when(has_left)
    def _():
        greet({"ctx": c - 1})

    @pl.when(has_right)
    def _():
        greet({"ctx": c + 1})

    greet({"head": sibling})
    for step in range(1, chips):
        greet({"head": other_chip(step) * 2 + core})

    def starts(place):
        first, end = jnp.zeros_like(place), 0
        for d in range(lengths_ref.shape[0]):
            end = end + lengths_ref[d]
            first = jnp.where(place >= end, end, first)
        return first

    for side, block in ((0, low_block), (1, high_block)):
        lane = lax.broadcasted_iota(jnp.int32, (1, half), 1)
        row_first = starts(block * half + lane)
        first_ref[side] = jnp.concatenate([row_first] * group, axis=1)
    lane = lax.broadcasted_iota(jnp.int32, (half, HD), 1)
    on_left = lane < HD // 2
    place = jnp.where(on_left, low_block, high_block) * half + lax.broadcasted_iota(
        jnp.int32, (half, HD), 0
    )
    offset = (place - starts(place)).astype(jnp.float32)
    expo = (lane % (HD // 2)).astype(jnp.float32) * (2.0 / HD)
    angle = offset * jnp.exp(-math.log(500000.0) * expo)
    cosine, sine = jnp.cos(angle), jnp.sin(angle)
    cosine_over, sine_over = pltpu.roll(cosine, HD // 2, 1), pltpu.roll(sine, HD // 2, 1)
    cos_ref[0:half, :] = jnp.where(on_left, cosine, cosine_over)
    cos_ref[half:rows, :] = jnp.where(on_left, cosine_over, cosine)
    sin_ref[0:half, :] = jnp.where(on_left, -sine, sine_over)
    sin_ref[half:rows, :] = jnp.where(on_left, -sine_over, sine)

    kv_acc[...] = jnp.zeros_like(kv_acc)
    norm[...] = jnp.zeros_like(norm)

    def project_piece(k, carry):
        for copy in load_piece(k):
            copy.wait()
        cols = pl.ds(pl.multiple_of(k * piece, piece), piece)

        kv_acc[...] += jnp.dot(tok[:, cols], kvw[cols, :], preferred_element_type=jnp.float32)
        for r in range(0, rows, 64):
            wide = tok[r : r + 64, cols].astype(jnp.float32)
            sq = wide * wide
            part = sq[:, 0:HD]
            for s in range(1, piece // HD):
                part = part + sq[:, s * HD : (s + 1) * HD]
            norm[r : r + 64, :] += part
        return carry

    lax.fori_loop(0, pieces, project_piece, 0)
    load_q.start()
    load_o.start()
    mean = jnp.sum(norm[...], axis=1, keepdims=True) * (1.0 / depth)
    norm[...] = jnp.broadcast_to(lax.rsqrt(mean + 1e-05), norm.shape)
    for g in range(kv_heads):
        for side, block in ((0, low_block), (1, high_block)):
            at = slice(side * half, (side + 1) * half)
            raw = kv_acc[at, g * HD : (g + 1) * HD] * norm[at, :]
            keys[block, g] = rotated(raw, cos_ref[at, :], sin_ref[at, :]).astype(jnp.bfloat16)
            raw = kv_acc[at, k_cols + g * HD : k_cols + (g + 1) * HD] * norm[at, :]
            values[block, g] = raw.T.astype(jnp.bfloat16)

    def block_copies(block, way):
        target = {"ctx": c + 1 if way else c - 1}
        return [
            pltpu.make_async_remote_copy(
                src_ref=ref.at[block],
                dst_ref=ref.at[block],
                send_sem=kv_send.at[way, kind, block],
                recv_sem=kv_recv.at[kind, block],
                device_id=target,
                device_id_type=MESH,
            )
            for kind, ref in enumerate((keys, values))
        ]

    def send(block, way):
        for copy in block_copies(block, way):
            copy.start()

    def receive(block, passes, way):
        landing, onward = block_copies(block, 0), block_copies(block, way)
        for kind in range(2):
            landing[kind].wait_recv()

            @pl.when(passes)
            def _():
                onward[kind].start()

    greeted = 1 + (chips - 1) + has_left.astype(jnp.int32) + has_right.astype(jnp.int32)
    pl.semaphore_wait(barrier, greeted)

    @pl.when(has_right)
    def _():
        send(low_block, 1)

    @pl.when(has_left)
    def _():
        send(high_block, 0)

    load_q.wait()
    factor = math.log2(math.e) / math.sqrt(HD)
    tile = min(256, q_heads * HD)

    def project_query(t, carry):
        cols = pl.ds(pl.multiple_of(t * tile, tile), tile)
        raw = jnp.dot(tok[...], qw[:, cols], preferred_element_type=jnp.float32)
        for h in range(tile // HD):
            part = raw[:, h * HD : (h + 1) * HD] * (norm[...] * factor)
            turned = rotated(part, cos_ref[...], sin_ref[...]).astype(jnp.bfloat16)
            at_head = t * (tile // HD) + h
            g, j = lax.div(at_head, group), lax.rem(at_head, group)
            at = pl.ds(pl.multiple_of(j * half, half), half)
            for side in range(2):
                query[g, side, at, :] = turned[side * half : (side + 1) * half]
        return carry

    lax.fori_loop(0, q_heads * HD // tile, project_query, 0)

    def attend(side, block, diagonal):
        def one_group(g, carry):
            slot = side * kv_heads + g
            key_at = lax.broadcasted_iota(jnp.int32, (half, wide_rows), 0)
            allowed = key_at >= first_ref[side] - block * half
            if diagonal:
                row_at = lax.broadcasted_iota(jnp.int32, (1, wide_rows), 1) % half
                allowed = allowed & (key_at <= row_at)
            scores = lax.dot_general(
                keys[block, g], query[g, side], (((1,), (1,)), ((), ())),
                preferred_element_type=jnp.float32,
            )
            scores = jnp.where(allowed, scores, LOW)
            here = jnp.max(scores, axis=0, keepdims=True)
            if not diagonal:
                before = top[slot]
                here = jnp.maximum(before, here)
            expo = jnp.exp2(scores - here)
            summed = jnp.sum(expo, axis=0, keepdims=True)
            fresh = jnp.dot(
                values[block, g], expo.astype(jnp.bfloat16), preferred_element_type=jnp.float32
            )
            if not diagonal:
                shrink = jnp.exp2(before - here)
                summed = summed + total[slot] * shrink
                fresh = fresh + accum[slot] * shrink
            top[slot] = here
            total[slot] = summed
            accum[slot] = fresh
            return carry

        lax.fori_loop(0, kv_heads, one_group, 0)

    def sib_copy(side, x, t):
        return pltpu.make_async_remote_copy(
            src_ref=sib_out.at[side, x, t],
            dst_ref=sib_in.at[side, x, t],
            send_sem=sib_send.at[side, x, t],
            recv_sem=sib_recv.at[side, x, t],
            device_id={"head": sibling},
            device_id_type=MESH,
        )

    def far_copy(side, step, t):
        x = other_chip(step)
        return pltpu.make_async_remote_copy(
            src_ref=far_out.at[side, step - 1, t],
            dst_ref=far_in.at[side, step - 1, t],
            send_sem=far_send.at[side, step - 1, t],
            recv_sem=far_recv.at[side, step - 1, t],
            device_id={"head": x * 2 + core},
            device_id_type=MESH,
        )

    out_tile = sib_out.shape[4]
    out_tiles = sib_out.shape[2]

    def project_out(owner, t):
        start = pl.multiple_of(owner * width + t * out_tile, out_tile)
        return jnp.dot(
            attended[...], ow[:, pl.ds(start, out_tile)], preferred_element_type=jnp.float32
        )

    def finish(side):
        for g in range(kv_heads):
            slot = side * kv_heads + g
            result = accum[slot] * (1.0 / total[slot])
            for j in range(group):
                h = g * group + j
                part = result[:, j * half : (j + 1) * half]
                attended[:, h * HD : (h + 1) * HD] = part.T.astype(jnp.bfloat16)
        for step in list(range(1, chips)) + [0]:
            x = other_chip(step)

            def for_sibling(t, carry):
                sib_out[side, x, t] = project_out(x * 2 + 1 - core, t).astype(jnp.bfloat16)
                sib_copy(side, x, t).start()
                return carry

            def for_own(t, carry):
                part = project_out(x * 2 + core, t)
                if step:
                    sib_copy(side, x, t).wait_recv()
                    far_out[side, step - 1, t] = (
                        part + sib_in[side, x, t].astype(jnp.float32)
                    ).astype(jnp.bfloat16)
                    far_copy(side, step, t).start()
                else:
                    kept[side, t] = part
                return carry

            lax.fori_loop(0, out_tiles, for_sibling, 0)
            lax.fori_loop(0, out_tiles, for_own, 0)

    load_o.wait()
    last_right = jnp.maximum(c + 1, n - 1 - c)
    right_count = jnp.where(has_right, 2 * n - 1 - c - last_right, 0)

    def from_left(i):
        return (i >= 1) & (i <= c)

    def from_right(i):
        return (i >= 1) & (i <= right_count)

    def passes_right(i):
        return from_left(i) & has_right

    def passes_left(i):
        return from_right(i) & has_left & (2 * n - 1 - c - i >= n - c)

    last_pass = jnp.where(has_left, jnp.minimum(right_count, n - 1), 0)
    finish_turn = jnp.maximum(c, jnp.where(c < n - c, last_pass, right_count) - 1)

    def arrive(i):
        @pl.when(from_left(i))
        def _():
            receive(c - i, has_right, 1)

        @pl.when(from_right(i))
        def _():
            receive(2 * n - 1 - c - i, passes_left(i), 0)

        @pl.when((i == right_count) & has_left & (c >= n - c))
        def _():
            send(low_block, 0)

    arrive(0)

    def turn(i, carry):
        early = passes_right(i + 1) | passes_left(i + 1)

        @pl.when(early)
        def _():
            arrive(i + 1)

        @pl.when(i == 0)
        def _():
            attend(0, low_block, True)
            attend(1, high_block, True)

        @pl.when(from_left(i))
        def _():
            attend(0, c - i, False)

        @pl.when(i == finish_turn)
        def _():
            finish(0)

        @pl.when((i <= c) & (c - i >= n - 1 - c))
        def _():
            attend(1, c - i, False)

        @pl.when(from_right(i))
        def _():
            attend(1, 2 * n - 1 - c - i, False)

        @pl.when(jnp.logical_not(early))
        def _():
            arrive(i + 1)

        return carry

    lax.fori_loop(0, n + 1, turn, 0)
    finish(1)

    def result_copy(side, t):
        cols = pl.ds(pl.multiple_of(t * out_tile, out_tile), out_tile)
        at = slice(side * half, (side + 1) * half)
        return pltpu.make_async_copy(mixed.at[side, t], out_ref.at[at, cols], out_sem.at[side, t])

    for side in range(2):

        def add_up(t, carry):
            sib_copy(side, chip, t).wait_recv()
            summed = kept[side, t] + sib_in[side, chip, t].astype(jnp.float32)
            for step in range(1, chips):
                far_copy(side, step, t).wait_recv()
                summed = summed + far_in[side, step - 1, t].astype(jnp.float32)
            mixed[side, t] = summed.astype(jnp.bfloat16)
            result_copy(side, t).start()
            return carry

        lax.fori_loop(0, out_tiles, add_up, 0)

    def drain_out(t, carry):
        for side in range(2):
            result_copy(side, t).wait()
            for x in range(chips):
                sib_copy(side, x, t).wait_send()
            for step in range(1, chips):
                far_copy(side, step, t).wait_send()
        return carry

    lax.fori_loop(0, out_tiles, drain_out, 0)

    def drain(block, carry):
        @pl.when(has_right & (block <= c))
        def _():
            for copy in block_copies(block, 1):
                copy.wait_send()

        @pl.when(has_left & (block >= jnp.maximum(c, n - c)) & (block <= high_block))
        def _():
            for copy in block_copies(block, 0):
                copy.wait_send()

        return carry

    lax.fori_loop(0, 2 * n, drain, 0)


def hand_over(source, target, sem):
    part = source.shape[0] // 4
    copies = [
        pltpu.make_async_copy(
            source.at[i * part : (i + 1) * part], target.at[i * part : (i + 1) * part], sem.at[i]
        )
        for i in range(4)
    ]
    for copy in copies:
        copy.start()
    for copy in copies:
        copy.wait()


def shards(n, n_head, tokens, lengths, q_weight, k_weight, v_weight, o_weight):
    rows, depth = tokens.shape
    half = rows // 2
    q_cols, k_cols = q_weight.shape[1], k_weight.shape[1]
    q_heads, kv_heads = q_cols // HD, k_cols // HD
    chips = n_head // 2
    width = o_weight.shape[1] // n_head
    group = q_heads // kv_heads
    bf16, f32 = jnp.bfloat16, jnp.float32
    dma = pltpu.SemaphoreType.DMA
    far = max(chips - 1, 1)
    tile = min(256, width)
    tiles = width // tile
    hbm = pl.BlockSpec(memory_space=pl.ANY)
    computed = pl.pallas_call(
        functools.partial(kernel, n, n_head),
        out_shape=jax.ShapeDtypeStruct((rows, width), bf16),
        in_specs=[pl.BlockSpec(memory_space=pltpu.SMEM)] + [hbm] * 5,
        out_specs=hbm,
        scratch_shapes=[
            pltpu.VMEM((2, 1, group * half), jnp.int32),
            pltpu.VMEM((rows, HD), f32),
            pltpu.VMEM((rows, HD), f32),
            pltpu.VMEM((rows, depth), bf16),
            pltpu.VMEM((depth, q_cols), bf16),
            pltpu.VMEM((depth, 2 * k_cols), bf16),
            pltpu.VMEM(o_weight.shape, bf16),
            pltpu.VMEM((rows, 2 * k_cols), f32),
            pltpu.VMEM((rows, HD), f32),
            pltpu.VMEM((kv_heads, 2, group * half, HD), bf16),
            pltpu.VMEM((2 * n, kv_heads, half, HD), bf16),
            pltpu.VMEM((2 * n, kv_heads, HD, half), bf16),
            pltpu.VMEM((2 * kv_heads, 1, group * half), f32),
            pltpu.VMEM((2 * kv_heads, 1, group * half), f32),
            pltpu.VMEM((2 * kv_heads, HD, group * half), f32),
            pltpu.VMEM((half, q_cols), bf16),
            pltpu.VMEM((2, tiles, half, tile), f32),
            pltpu.VMEM((2, tiles, half, tile), bf16),
            pltpu.VMEM((2, chips, tiles, half, tile), bf16),
            pltpu.VMEM((2, chips, tiles, half, tile), bf16),
            pltpu.VMEM((2, far, tiles, half, tile), bf16),
            pltpu.VMEM((2, far, tiles, half, tile), bf16),
            dma((4,)), dma((4,)), dma((4,)), dma, dma,
            dma((2, 2, 2 * n)), dma((2, 2 * n)),
            dma((2, chips, tiles)), dma((2, chips, tiles)),
            dma((2, far, tiles)), dma((2, far, tiles)),
            dma((2, tiles)),
        ],
        compiler_params=pltpu.CompilerParams(
            collective_id=0, has_side_effects=True, vmem_limit_bytes=60 * 2**20
        ),
    )(lengths, tokens, q_weight, k_weight, v_weight, o_weight)
    return pl.pallas_call(
        hand_over,
        out_shape=jax.ShapeDtypeStruct((rows, width), bf16),
        in_specs=[hbm],
        out_specs=hbm,
        scratch_shapes=[dma((4,))],
    )(computed)


def solution(mesh):
    return jax.shard_map(
        functools.partial(shards, mesh.shape["ctx"], mesh.shape["head"]),
        mesh=mesh,
        in_specs=(
            P(("groups", "ctx"), None),
            P("groups"),
            P(None, "head"),
            P(None, "head"),
            P(None, "head"),
            P("head", None),
        ),
        out_specs=P(("groups", "ctx"), "head"),
        check_vma=False,
    )
```

```python
import functools
import math

import jax
import jax.numpy as jnp
from jax import lax
from jax.experimental import pallas as pl
from jax.experimental.pallas import tpu as pltpu
from jax.sharding import PartitionSpec as P

HD = 128
MESH = pl.DeviceIdType.MESH
LOW = -1e30


def rotated(values, cosine, sine):
    return values * cosine + pltpu.roll(values, HD // 2, 1) * sine


def kernel(
    n, n_head, lengths_ref, tok_hbm, qw_hbm, kw_hbm, vw_hbm, ow_hbm,
    out_ref,
    first_ref, cos_ref, sin_ref, tok, qw, kvw, ow, kv_acc, norm, query, keys, values, top, total, accum, attended,
    kept, mixed, sib_out, sib_in, far_out, far_in,
    tok_sem, kw_sem, vw_sem, qw_sem, ow_sem,
    kv_send, kv_recv, sib_send, sib_recv, far_send, far_recv, out_sem,
):
    rows, depth = tok.shape
    half = rows // 2
    kv_heads = keys.shape[1]
    group = query.shape[2] // half
    q_heads = kv_heads * group
    wide_rows = group * half
    k_cols = kv_heads * HD
    chips = n_head // 2
    width = out_ref.shape[1]
    pieces = 4
    piece = depth // pieces

    c = lax.axis_index("ctx")
    head = lax.axis_index("head")
    chip, core = lax.div(head, 2), lax.rem(head, 2)
    sibling = chip * 2 + 1 - core
    has_left, has_right = c > 0, c < n - 1
    low_block, high_block = c, 2 * n - 1 - c

    def other_chip(step):
        return lax.rem(chip + step, chips)

    def load_piece(k):
        cols = pl.ds(pl.multiple_of(k * piece, piece), piece)
        return (
            pltpu.make_async_copy(tok_hbm.at[:, cols], tok.at[:, cols], tok_sem.at[k]),
            pltpu.make_async_copy(kw_hbm.at[cols, :], kvw.at[cols, 0:k_cols], kw_sem.at[k]),
            pltpu.make_async_copy(
                vw_hbm.at[cols, :], kvw.at[cols, k_cols : 2 * k_cols], vw_sem.at[k]
            ),
        )

    for k in range(pieces):
        for copy in load_piece(k):
            copy.start()
    load_q = pltpu.make_async_copy(qw_hbm, qw, qw_sem)
    load_o = pltpu.make_async_copy(ow_hbm, ow, ow_sem)

    barrier = pltpu.get_barrier_semaphore()

    def greet(target):
        pl.semaphore_signal(barrier, inc=1, device_id=target, device_id_type=MESH)

    reaches = range(1, n, 2)
    for reach in reaches:

        @pl.when(c >= reach)
        def _():
            greet({"ctx": c - reach})

    @pl.when(has_right)
    def _():
        greet({"ctx": c + 1})

    greet({"head": sibling})
    for step in range(1, chips):
        greet({"head": other_chip(step) * 2 + core})

    def starts(place):
        first, end = jnp.zeros_like(place), 0
        for d in range(lengths_ref.shape[0]):
            end = end + lengths_ref[d]
            first = jnp.where(place >= end, end, first)
        return first

    for side, block in ((0, low_block), (1, high_block)):
        lane = lax.broadcasted_iota(jnp.int32, (1, half), 1)
        row_first = starts(block * half + lane)
        first_ref[side] = jnp.concatenate([row_first] * group, axis=1)
    lane = lax.broadcasted_iota(jnp.int32, (half, HD), 1)
    on_left = lane < HD // 2
    place = jnp.where(on_left, low_block, high_block) * half + lax.broadcasted_iota(
        jnp.int32, (half, HD), 0
    )
    offset = (place - starts(place)).astype(jnp.float32)
    expo = (lane % (HD // 2)).astype(jnp.float32) * (2.0 / HD)
    angle = offset * jnp.exp(-math.log(500000.0) * expo)
    cosine, sine = jnp.cos(angle), jnp.sin(angle)
    cosine_over, sine_over = pltpu.roll(cosine, HD // 2, 1), pltpu.roll(sine, HD // 2, 1)
    cos_ref[0:half, :] = jnp.where(on_left, cosine, cosine_over)
    cos_ref[half:rows, :] = jnp.where(on_left, cosine_over, cosine)
    sin_ref[0:half, :] = jnp.where(on_left, -sine, sine_over)
    sin_ref[half:rows, :] = jnp.where(on_left, -sine_over, sine)

    kv_acc[...] = jnp.zeros_like(kv_acc)
    norm[...] = jnp.zeros_like(norm)

    def project_piece(k, carry):
        for copy in load_piece(k):
            copy.wait()
        cols = pl.ds(pl.multiple_of(k * piece, piece), piece)

        kv_acc[...] += jnp.dot(tok[:, cols], kvw[cols, :], preferred_element_type=jnp.float32)
        for r in range(0, rows, 64):
            wide = tok[r : r + 64, cols].astype(jnp.float32)
            sq = wide * wide
            part = sq[:, 0:HD]
            for s in range(1, piece // HD):
                part = part + sq[:, s * HD : (s + 1) * HD]
            norm[r : r + 64, :] += part
        return carry

    lax.fori_loop(0, pieces, project_piece, 0)
    load_q.start()
    load_o.start()
    mean = jnp.sum(norm[...], axis=1, keepdims=True) * (1.0 / depth)
    norm[...] = jnp.broadcast_to(lax.rsqrt(mean + 1e-05), norm.shape)
    for g in range(kv_heads):
        for side, block in ((0, low_block), (1, high_block)):
            at = slice(side * half, (side + 1) * half)
            raw = kv_acc[at, g * HD : (g + 1) * HD] * norm[at, :]
            keys[block, g] = rotated(raw, cos_ref[at, :], sin_ref[at, :]).astype(jnp.bfloat16)
            raw = kv_acc[at, k_cols + g * HD : k_cols + (g + 1) * HD] * norm[at, :]
            values[block, g] = raw.T.astype(jnp.bfloat16)

    def block_copies(block, way):
        target = {"ctx": c + 2 * way - 1}
        return [
            pltpu.make_async_remote_copy(
                src_ref=ref.at[block],
                dst_ref=ref.at[block],
                send_sem=kv_send.at[way, kind, block],
                recv_sem=kv_recv.at[kind, block],
                device_id=target,
                device_id_type=MESH,
            )
            for kind, ref in enumerate((keys, values))
        ]

    def send(block, way):
        for copy in block_copies(block, way):
            copy.start()

    def receive(block, passes, way):
        landing, onward = block_copies(block, 0), block_copies(block, way)
        for kind in range(2):
            landing[kind].wait_recv()

            @pl.when(passes)
            def _():
                onward[kind].start()

    greeted = 1 + (chips - 1) + has_left.astype(jnp.int32)
    for reach in reaches:
        greeted = greeted + (c + reach < n).astype(jnp.int32)
    pl.semaphore_wait(barrier, greeted)

    @pl.when(has_left)
    def _():
        send(high_block, 0)

    for reach in reaches:

        @pl.when(c + reach < n)
        def _():
            send(low_block, (reach + 1) // 2)

    load_q.wait()
    factor = math.log2(math.e) / math.sqrt(HD)
    tile = min(256, q_heads * HD)

    def project_query(t, carry):
        cols = pl.ds(pl.multiple_of(t * tile, tile), tile)
        raw = jnp.dot(tok[...], qw[:, cols], preferred_element_type=jnp.float32)
        for h in range(tile // HD):
            part = raw[:, h * HD : (h + 1) * HD] * (norm[...] * factor)
            turned = rotated(part, cos_ref[...], sin_ref[...]).astype(jnp.bfloat16)
            at_head = t * (tile // HD) + h
            g, j = lax.div(at_head, group), lax.rem(at_head, group)
            at = pl.ds(pl.multiple_of(j * half, half), half)
            for side in range(2):
                query[g, side, at, :] = turned[side * half : (side + 1) * half]
        return carry

    lax.fori_loop(0, q_heads * HD // tile, project_query, 0)

    def attend(side, block, diagonal):
        def one_group(g, carry):
            slot = side * kv_heads + g
            key_at = lax.broadcasted_iota(jnp.int32, (half, wide_rows), 0)
            allowed = key_at >= first_ref[side] - block * half
            if diagonal:
                row_at = lax.broadcasted_iota(jnp.int32, (1, wide_rows), 1) % half
                allowed = allowed & (key_at <= row_at)
            scores = lax.dot_general(
                keys[block, g], query[g, side], (((1,), (1,)), ((), ())),
                preferred_element_type=jnp.float32,
            )
            scores = jnp.where(allowed, scores, LOW)
            here = jnp.max(scores, axis=0, keepdims=True)
            if not diagonal:
                before = top[slot]
                here = jnp.maximum(before, here)
            expo = jnp.exp2(scores - here)
            summed = jnp.sum(expo, axis=0, keepdims=True)
            fresh = jnp.dot(
                values[block, g], expo.astype(jnp.bfloat16), preferred_element_type=jnp.float32
            )
            if not diagonal:
                shrink = jnp.exp2(before - here)
                summed = summed + total[slot] * shrink
                fresh = fresh + accum[slot] * shrink
            top[slot] = here
            total[slot] = summed
            accum[slot] = fresh
            return carry

        lax.fori_loop(0, kv_heads, one_group, 0)

    def sib_copy(side, x, t):
        return pltpu.make_async_remote_copy(
            src_ref=sib_out.at[side, x, t],
            dst_ref=sib_in.at[side, x, t],
            send_sem=sib_send.at[side, x, t],
            recv_sem=sib_recv.at[side, x, t],
            device_id={"head": sibling},
            device_id_type=MESH,
        )

    def far_copy(side, step, t):
        x = other_chip(step)
        return pltpu.make_async_remote_copy(
            src_ref=far_out.at[side, step - 1, t],
            dst_ref=far_in.at[side, step - 1, t],
            send_sem=far_send.at[side, step - 1, t],
            recv_sem=far_recv.at[side, step - 1, t],
            device_id={"head": x * 2 + core},
            device_id_type=MESH,
        )

    out_tile = sib_out.shape[4]
    out_tiles = sib_out.shape[2]

    def project_out(owner, t):
        start = pl.multiple_of(owner * width + t * out_tile, out_tile)
        return jnp.dot(
            attended[...], ow[:, pl.ds(start, out_tile)], preferred_element_type=jnp.float32
        )

    def finish(side):
        for g in range(kv_heads):
            slot = side * kv_heads + g
            result = accum[slot] * (1.0 / total[slot])
            for j in range(group):
                h = g * group + j
                part = result[:, j * half : (j + 1) * half]
                attended[:, h * HD : (h + 1) * HD] = part.T.astype(jnp.bfloat16)
        for step in list(range(1, chips)) + [0]:
            x = other_chip(step)

            def for_sibling(t, carry):
                sib_out[side, x, t] = project_out(x * 2 + 1 - core, t).astype(jnp.bfloat16)
                sib_copy(side, x, t).start()
                return carry

            def for_own(t, carry):
                part = project_out(x * 2 + core, t)
                if step:
                    sib_copy(side, x, t).wait_recv()
                    far_out[side, step - 1, t] = (
                        part + sib_in[side, x, t].astype(jnp.float32)
                    ).astype(jnp.bfloat16)
                    far_copy(side, step, t).start()
                else:
                    kept[side, t] = part
                return carry

            lax.fori_loop(0, out_tiles, for_sibling, 0)
            lax.fori_loop(0, out_tiles, for_own, 0)

    load_o.wait()
    last_right = jnp.maximum(c + 1, n - 1 - c)
    right_count = jnp.where(has_right, 2 * n - 1 - c - last_right, 0)

    def from_left(i):
        return (i >= 1) & (i <= c)

    def from_right(i):
        return (i >= 1) & (i <= right_count)

    def passes_left(i):
        return from_right(i) & has_left & (2 * n - 1 - c - i >= n - c)

    last_pass = jnp.where(has_left, jnp.minimum(right_count, n - 1), 0)
    finish_turn = jnp.maximum(c, jnp.where(c < n - c, last_pass, right_count) - 1)

    def arrive_left(i):
        @pl.when(from_left(i))
        def _():
            receive(c - i, has_right & (i % 2 == 1), 1)

    def arrive_right(i):
        @pl.when(from_right(i))
        def _():
            receive(2 * n - 1 - c - i, passes_left(i), 0)

        @pl.when((i == right_count) & has_left & (c >= n - c))
        def _():
            send(low_block, 0)

    arrive_right(0)

    def turn(i, carry):
        @pl.when(passes_left(i + 1))
        def _():
            arrive_right(i + 1)

        @pl.when(i == 0)
        def _():
            attend(0, low_block, True)
            attend(1, high_block, True)

        @pl.when(from_left(i))
        def _():
            attend(0, c - i, False)

        @pl.when(i == finish_turn)
        def _():
            finish(0)

        @pl.when((i <= c) & (c - i >= n - 1 - c))
        def _():
            attend(1, c - i, False)

        @pl.when(from_right(i))
        def _():
            attend(1, 2 * n - 1 - c - i, False)

        @pl.when(jnp.logical_not(passes_left(i + 1)))
        def _():
            arrive_right(i + 1)

        arrive_left(i + 1)

        return carry

    lax.fori_loop(0, n + 1, turn, 0)
    finish(1)

    def result_copy(side, t):
        cols = pl.ds(pl.multiple_of(t * out_tile, out_tile), out_tile)
        at = slice(side * half, (side + 1) * half)
        return pltpu.make_async_copy(mixed.at[side, t], out_ref.at[at, cols], out_sem.at[side, t])

    for side in range(2):

        def add_up(t, carry):
            sib_copy(side, chip, t).wait_recv()
            summed = kept[side, t] + sib_in[side, chip, t].astype(jnp.float32)
            for step in range(1, chips):
                far_copy(side, step, t).wait_recv()
                summed = summed + far_in[side, step - 1, t].astype(jnp.float32)
            mixed[side, t] = summed.astype(jnp.bfloat16)
            result_copy(side, t).start()
            return carry

        lax.fori_loop(0, out_tiles, add_up, 0)

    def drain_out(t, carry):
        for side in range(2):
            result_copy(side, t).wait()
            for x in range(chips):
                sib_copy(side, x, t).wait_send()
            for step in range(1, chips):
                far_copy(side, step, t).wait_send()
        return carry

    lax.fori_loop(0, out_tiles, drain_out, 0)

    def drain(block, carry):
        @pl.when(has_right & ((block == c) | ((block < c) & ((c - block) % 2 == 1))))
        def _():
            for copy in block_copies(block, 1):
                copy.wait_send()

        @pl.when(has_left & (block >= jnp.maximum(c, n - c)) & (block <= high_block))
        def _():
            for copy in block_copies(block, 0):
                copy.wait_send()

        return carry

    lax.fori_loop(0, 2 * n, drain, 0)
    for reach in reaches[1:]:

        @pl.when(c + reach < n)
        def _():
            for copy in block_copies(low_block, (reach + 1) // 2):
                copy.wait_send()


def hand_over(source, target):
    target[...] = source[...]


def shards(n, n_head, tokens, lengths, q_weight, k_weight, v_weight, o_weight):
    rows, depth = tokens.shape
    half = rows // 2
    q_cols, k_cols = q_weight.shape[1], k_weight.shape[1]
    q_heads, kv_heads = q_cols // HD, k_cols // HD
    chips = n_head // 2
    width = o_weight.shape[1] // n_head
    group = q_heads // kv_heads
    bf16, f32 = jnp.bfloat16, jnp.float32
    dma = pltpu.SemaphoreType.DMA
    far = max(chips - 1, 1)
    tile = min(256, width)
    tiles = width // tile
    hbm = pl.BlockSpec(memory_space=pl.ANY)
    computed = pl.pallas_call(
        functools.partial(kernel, n, n_head),
        out_shape=jax.ShapeDtypeStruct((rows, width), bf16),
        in_specs=[pl.BlockSpec(memory_space=pltpu.SMEM)] + [hbm] * 5,
        out_specs=hbm,
        scratch_shapes=[
            pltpu.VMEM((2, 1, group * half), jnp.int32),
            pltpu.VMEM((rows, HD), f32),
            pltpu.VMEM((rows, HD), f32),
            pltpu.VMEM((rows, depth), bf16),
            pltpu.VMEM((depth, q_cols), bf16),
            pltpu.VMEM((depth, 2 * k_cols), bf16),
            pltpu.VMEM(o_weight.shape, bf16),
            pltpu.VMEM((rows, 2 * k_cols), f32),
            pltpu.VMEM((rows, HD), f32),
            pltpu.VMEM((kv_heads, 2, group * half, HD), bf16),
            pltpu.VMEM((2 * n, kv_heads, half, HD), bf16),
            pltpu.VMEM((2 * n, kv_heads, HD, half), bf16),
            pltpu.VMEM((2 * kv_heads, 1, group * half), f32),
            pltpu.VMEM((2 * kv_heads, 1, group * half), f32),
            pltpu.VMEM((2 * kv_heads, HD, group * half), f32),
            pltpu.VMEM((half, q_cols), bf16),
            pltpu.VMEM((2, tiles, half, tile), f32),
            pltpu.VMEM((2, tiles, half, tile), bf16),
            pltpu.VMEM((2, chips, tiles, half, tile), bf16),
            pltpu.VMEM((2, chips, tiles, half, tile), bf16),
            pltpu.VMEM((2, far, tiles, half, tile), bf16),
            pltpu.VMEM((2, far, tiles, half, tile), bf16),
            dma((4,)), dma((4,)), dma((4,)), dma, dma,
            dma((1 + n // 2, 2, 2 * n)), dma((2, 2 * n)),
            dma((2, chips, tiles)), dma((2, chips, tiles)),
            dma((2, far, tiles)), dma((2, far, tiles)),
            dma((2, tiles)),
        ],
        compiler_params=pltpu.CompilerParams(
            collective_id=0, has_side_effects=True, vmem_limit_bytes=60 * 2**20
        ),
    )(lengths, tokens, q_weight, k_weight, v_weight, o_weight)
    return pl.pallas_call(
        hand_over,
        out_shape=jax.ShapeDtypeStruct((rows, width), bf16),
        grid=(4,),
        in_specs=[pl.BlockSpec((rows // 4, width), lambda i: (i, 0))],
        out_specs=pl.BlockSpec((rows // 4, width), lambda i: (i, 0)),
    )(computed)


def solution(mesh):
    return jax.shard_map(
        functools.partial(shards, mesh.shape["ctx"], mesh.shape["head"]),
        mesh=mesh,
        in_specs=(
            P(("groups", "ctx"), None),
            P("groups"),
            P(None, "head"),
            P(None, "head"),
            P(None, "head"),
            P("head", None),
        ),
        out_specs=P(("groups", "ctx"), "head"),
        check_vma=False,
    )
```

```python
import functools
import math

import jax
import jax.numpy as jnp
from jax import lax
from jax.experimental import pallas as pl
from jax.experimental.pallas import tpu as pltpu
from jax.sharding import PartitionSpec as P

HD = 128
MESH = pl.DeviceIdType.MESH
LOW = -1e30


def rotated(values, cosine, sine):
    return values * cosine + pltpu.roll(values, HD // 2, 1) * sine


def kernel(
    n, n_head, lengths_ref, tok_hbm, qw_hbm, kw_hbm, vw_hbm, ow_hbm,
    near_ref, far_ref,
    first_ref, cos_ref, sin_ref, tok, qw, kvw, ow, kv_acc, norm, query, keys, values, top, total, accum, attended,
    kept, near, sib_out, sib_in, far_out,
    tok_sem, kw_sem, vw_sem, qw_sem, ow_sem,
    kv_send, kv_recv, sib_send, sib_recv, far_send, far_recv, out_sem,
):
    rows, depth = tok.shape
    half = rows // 2
    kv_heads = keys.shape[1]
    group = query.shape[2] // half
    q_heads = kv_heads * group
    wide_rows = group * half
    k_cols = kv_heads * HD
    chips = n_head // 2
    width = near_ref.shape[1]
    pieces = 4
    piece = depth // pieces

    c = lax.axis_index("ctx")
    head = lax.axis_index("head")
    chip, core = lax.div(head, 2), lax.rem(head, 2)
    sibling = chip * 2 + 1 - core
    has_left, has_right = c > 0, c < n - 1
    low_block, high_block = c, 2 * n - 1 - c

    def other_chip(step):
        return lax.rem(chip + step, chips)

    def load_piece(k):
        cols = pl.ds(pl.multiple_of(k * piece, piece), piece)
        return (
            pltpu.make_async_copy(tok_hbm.at[:, cols], tok.at[:, cols], tok_sem.at[k]),
            pltpu.make_async_copy(kw_hbm.at[cols, :], kvw.at[cols, 0:k_cols], kw_sem.at[k]),
            pltpu.make_async_copy(
                vw_hbm.at[cols, :], kvw.at[cols, k_cols : 2 * k_cols], vw_sem.at[k]
            ),
        )

    for k in range(pieces):
        for copy in load_piece(k):
            copy.start()
    load_q = pltpu.make_async_copy(qw_hbm, qw, qw_sem)
    load_o = pltpu.make_async_copy(ow_hbm, ow, ow_sem)

    barrier = pltpu.get_barrier_semaphore()

    def greet(target):
        pl.semaphore_signal(barrier, inc=1, device_id=target, device_id_type=MESH)

    reaches = range(1, n, 2)
    for reach in reaches:

        @pl.when(c >= reach)
        def _():
            greet({"ctx": c - reach})

    @pl.when(has_right)
    def _():
        greet({"ctx": c + 1})

    greet({"head": sibling})
    for step in range(1, chips):
        greet({"head": other_chip(step) * 2 + core})

    def starts(place):
        first, end = jnp.zeros_like(place), 0
        for d in range(lengths_ref.shape[0]):
            end = end + lengths_ref[d]
            first = jnp.where(place >= end, end, first)
        return first

    for side, block in ((0, low_block), (1, high_block)):
        lane = lax.broadcasted_iota(jnp.int32, (1, half), 1)
        row_first = starts(block * half + lane)
        first_ref[side] = jnp.concatenate([row_first] * group, axis=1)
    lane = lax.broadcasted_iota(jnp.int32, (half, HD), 1)
    on_left = lane < HD // 2
    place = jnp.where(on_left, low_block, high_block) * half + lax.broadcasted_iota(
        jnp.int32, (half, HD), 0
    )
    offset = (place - starts(place)).astype(jnp.float32)
    expo = (lane % (HD // 2)).astype(jnp.float32) * (2.0 / HD)
    angle = offset * jnp.exp(-math.log(500000.0) * expo)
    cosine, sine = jnp.cos(angle), jnp.sin(angle)
    cosine_over, sine_over = pltpu.roll(cosine, HD // 2, 1), pltpu.roll(sine, HD // 2, 1)
    cos_ref[0:half, :] = jnp.where(on_left, cosine, cosine_over)
    cos_ref[half:rows, :] = jnp.where(on_left, cosine_over, cosine)
    sin_ref[0:half, :] = jnp.where(on_left, -sine, sine_over)
    sin_ref[half:rows, :] = jnp.where(on_left, -sine_over, sine)

    kv_acc[...] = jnp.zeros_like(kv_acc)
    norm[...] = jnp.zeros_like(norm)

    def project_piece(k, carry):
        for copy in load_piece(k):
            copy.wait()

        @pl.when(k == pieces // 2)
        def _():
            load_q.start()

        cols = pl.ds(pl.multiple_of(k * piece, piece), piece)

        kv_acc[...] += jnp.dot(tok[:, cols], kvw[cols, :], preferred_element_type=jnp.float32)
        for r in range(0, rows, 64):
            wide = tok[r : r + 64, cols].astype(jnp.float32)
            sq = wide * wide
            part = sq[:, 0:HD]
            for s in range(1, piece // HD):
                part = part + sq[:, s * HD : (s + 1) * HD]
            norm[r : r + 64, :] += part
        return carry

    lax.fori_loop(0, pieces, project_piece, 0)
    mean = jnp.sum(norm[...], axis=1, keepdims=True) * (1.0 / depth)
    norm[...] = jnp.broadcast_to(lax.rsqrt(mean + 1e-05), norm.shape)
    for g in range(kv_heads):
        for side, block in ((0, low_block), (1, high_block)):
            at = slice(side * half, (side + 1) * half)
            raw = kv_acc[at, g * HD : (g + 1) * HD] * norm[at, :]
            keys[block, g] = rotated(raw, cos_ref[at, :], sin_ref[at, :]).astype(jnp.bfloat16)
            raw = kv_acc[at, k_cols + g * HD : k_cols + (g + 1) * HD] * norm[at, :]
            values[block, g] = raw.T.astype(jnp.bfloat16)

    def block_copies(block, way):
        target = {"ctx": c + 2 * way - 1}
        return [
            pltpu.make_async_remote_copy(
                src_ref=ref.at[block],
                dst_ref=ref.at[block],
                send_sem=kv_send.at[way, kind, block],
                recv_sem=kv_recv.at[kind, block],
                device_id=target,
                device_id_type=MESH,
            )
            for kind, ref in enumerate((keys, values))
        ]

    def send(block, way):
        for copy in block_copies(block, way):
            copy.start()

    def receive(block, passes, way):
        landing, onward = block_copies(block, 0), block_copies(block, way)
        for kind in range(2):
            landing[kind].wait_recv()

            @pl.when(passes)
            def _():
                onward[kind].start()

    greeted = 1 + (chips - 1) + has_left.astype(jnp.int32)
    for reach in reaches:
        greeted = greeted + (c + reach < n).astype(jnp.int32)
    pl.semaphore_wait(barrier, greeted)

    @pl.when(has_left)
    def _():
        send(high_block, 0)

    for reach in reaches:

        @pl.when(c + reach < n)
        def _():
            send(low_block, (reach + 1) // 2)

    load_q.wait()
    load_o.start()
    factor = math.log2(math.e) / math.sqrt(HD)
    tile = min(256, q_heads * HD)

    def project_query(t, carry):
        cols = pl.ds(pl.multiple_of(t * tile, tile), tile)
        raw = jnp.dot(tok[...], qw[:, cols], preferred_element_type=jnp.float32)
        for h in range(tile // HD):
            part = raw[:, h * HD : (h + 1) * HD] * (norm[...] * factor)
            turned = rotated(part, cos_ref[...], sin_ref[...]).astype(jnp.bfloat16)
            at_head = t * (tile // HD) + h
            g, j = lax.div(at_head, group), lax.rem(at_head, group)
            at = pl.ds(pl.multiple_of(j * half, half), half)
            for side in range(2):
                query[g, side, at, :] = turned[side * half : (side + 1) * half]
        return carry

    lax.fori_loop(0, q_heads * HD // tile, project_query, 0)

    def attend(side, block, diagonal):
        def one_group(g, carry):
            slot = side * kv_heads + g
            key_at = lax.broadcasted_iota(jnp.int32, (half, wide_rows), 0)
            allowed = key_at >= first_ref[side] - block * half
            if diagonal:
                row_at = lax.broadcasted_iota(jnp.int32, (1, wide_rows), 1) % half
                allowed = allowed & (key_at <= row_at)
            scores = lax.dot_general(
                keys[block, g], query[g, side], (((1,), (1,)), ((), ())),
                preferred_element_type=jnp.float32,
            )
            scores = jnp.where(allowed, scores, LOW)
            here = jnp.max(scores, axis=0, keepdims=True)
            if not diagonal:
                before = top[slot]
                here = jnp.maximum(before, here)
            expo = jnp.exp2(scores - here)
            summed = jnp.sum(expo, axis=0, keepdims=True)
            fresh = jnp.dot(
                values[block, g], expo.astype(jnp.bfloat16), preferred_element_type=jnp.float32
            )
            if not diagonal:
                shrink = jnp.exp2(before - here)
                summed = summed + total[slot] * shrink
                fresh = fresh + accum[slot] * shrink
            top[slot] = here
            total[slot] = summed
            accum[slot] = fresh
            return carry

        lax.fori_loop(0, kv_heads, one_group, 0)

    def sib_copy(side, x, t):
        return pltpu.make_async_remote_copy(
            src_ref=sib_out.at[side, x, t],
            dst_ref=sib_in.at[side, x, t],
            send_sem=sib_send.at[side, x, t],
            recv_sem=sib_recv.at[side, x, t],
            device_id={"head": sibling},
            device_id_type=MESH,
        )

    def tile_of(side, t):
        cols = pl.ds(pl.multiple_of(t * out_tile, out_tile), out_tile)
        return pl.ds(side * half, half), cols

    def far_copy(side, step, t):
        x = other_chip(step)
        return pltpu.make_async_remote_copy(
            src_ref=far_out.at[side, step - 1, t],
            dst_ref=far_ref.at[step - 1, *tile_of(side, t)],
            send_sem=far_send.at[side, step - 1, t],
            recv_sem=far_recv.at[side, step - 1, t],
            device_id={"head": x * 2 + core},
            device_id_type=MESH,
        )

    out_tile = sib_out.shape[4]
    out_tiles = sib_out.shape[2]

    def project_out(owner, t):
        start = pl.multiple_of(owner * width + t * out_tile, out_tile)
        return jnp.dot(
            attended[...], ow[:, pl.ds(start, out_tile)], preferred_element_type=jnp.float32
        )

    def finish(side):
        for g in range(kv_heads):
            slot = side * kv_heads + g
            result = accum[slot] * (1.0 / total[slot])
            for j in range(group):
                h = g * group + j
                part = result[:, j * half : (j + 1) * half]
                attended[:, h * HD : (h + 1) * HD] = part.T.astype(jnp.bfloat16)
        for step in list(range(1, chips)) + [0]:
            x = other_chip(step)

            def for_sibling(t, carry):
                sib_out[side, x, t] = project_out(x * 2 + 1 - core, t).astype(jnp.bfloat16)
                sib_copy(side, x, t).start()
                return carry

            def for_own(t, carry):
                part = project_out(x * 2 + core, t)
                if step:
                    sib_copy(side, x, t).wait_recv()
                    far_out[side, step - 1, t] = (
                        part + sib_in[side, x, t].astype(jnp.float32)
                    ).astype(jnp.bfloat16)
                    far_copy(side, step, t).start()
                else:
                    kept[side, t] = part
                return carry

            lax.fori_loop(0, out_tiles, for_sibling, 0)
            lax.fori_loop(0, out_tiles, for_own, 0)

    load_o.wait()
    last_right = jnp.maximum(c + 1, n - 1 - c)
    right_count = jnp.where(has_right, 2 * n - 1 - c - last_right, 0)

    def from_left(i):
        return (i >= 1) & (i <= c)

    def from_right(i):
        return (i >= 1) & (i <= right_count)

    def passes_left(i):
        return from_right(i) & has_left & (2 * n - 1 - c - i >= n - c)

    last_pass = jnp.where(has_left, jnp.minimum(right_count, n - 1), 0)
    finish_turn = jnp.maximum(c, jnp.where(c < n - c, last_pass, right_count) - 1)

    def arrive_left(i):
        @pl.when(from_left(i))
        def _():
            receive(c - i, has_right & (i % 2 == 1), 1)

    def arrive_right(i):
        @pl.when(from_right(i))
        def _():
            receive(2 * n - 1 - c - i, passes_left(i), 0)

    sends_low = has_left & (c >= n - c)

    @pl.when(sends_low & (right_count == 0))
    def _():
        send(low_block, 0)

    def turn(i, carry):
        @pl.when(passes_left(i + 1))
        def _():
            arrive_right(i + 1)

        @pl.when(i == 0)
        def _():
            attend(0, low_block, True)
            attend(1, high_block, True)

        @pl.when(from_left(i))
        def _():
            attend(0, c - i, False)

        @pl.when(i == finish_turn)
        def _():
            finish(0)

        @pl.when((i <= c) & (c - i >= n - 1 - c) & (has_right | (i == 0)))
        def _():
            attend(1, c - i, False)

        @pl.when(from_right(i))
        def _():
            attend(1, 2 * n - 1 - c - i, False)

        @pl.when(jnp.logical_not(passes_left(i + 1)))
        def _():
            arrive_right(i + 1)

        @pl.when(sends_low & (i + 1 == right_count))
        def _():
            send(low_block, 0)

        arrive_left(i + 1)
        return carry

    lax.fori_loop(0, n + 1, turn, 0)

    @pl.when(jnp.logical_not(has_right))
    def _():
        def put_off(block, carry):
            attend(1, block, False)
            return carry

        lax.fori_loop(0, n - 1, put_off, 0)

    finish(1)

    def near_copy(side, t):
        return pltpu.make_async_copy(
            near.at[side, t], near_ref.at[*tile_of(side, t)], out_sem.at[side, t]
        )

    for side in range(2):

        def add_up(t, carry):
            sib_copy(side, chip, t).wait_recv()
            summed = kept[side, t] + sib_in[side, chip, t].astype(jnp.float32)
            near[side, t] = summed.astype(jnp.bfloat16)
            near_copy(side, t).start()
            return carry

        lax.fori_loop(0, out_tiles, add_up, 0)

    def drain_out(t, carry):
        for side in range(2):
            near_copy(side, t).wait()
            for x in range(chips):
                sib_copy(side, x, t).wait_send()
            for step in range(1, chips):
                far_copy(side, step, t).wait()
        return carry

    lax.fori_loop(0, out_tiles, drain_out, 0)

    def drain(block, carry):
        @pl.when(has_right & ((block == c) | ((block < c) & ((c - block) % 2 == 1))))
        def _():
            for copy in block_copies(block, 1):
                copy.wait_send()

        @pl.when(has_left & (block >= jnp.maximum(c, n - c)) & (block <= high_block))
        def _():
            for copy in block_copies(block, 0):
                copy.wait_send()

        return carry

    lax.fori_loop(0, 2 * n, drain, 0)
    for reach in reaches[1:]:

        @pl.when(c + reach < n)
        def _():
            for copy in block_copies(low_block, (reach + 1) // 2):
                copy.wait_send()


def shards(n, n_head, tokens, lengths, q_weight, k_weight, v_weight, o_weight):
    rows, depth = tokens.shape
    half = rows // 2
    q_cols, k_cols = q_weight.shape[1], k_weight.shape[1]
    q_heads, kv_heads = q_cols // HD, k_cols // HD
    chips = n_head // 2
    width = o_weight.shape[1] // n_head
    group = q_heads // kv_heads
    bf16, f32 = jnp.bfloat16, jnp.float32
    dma = pltpu.SemaphoreType.DMA
    far = max(chips - 1, 1)
    tile = min(256, width)
    tiles = width // tile
    hbm = pl.BlockSpec(memory_space=pl.ANY)
    near, others = pl.pallas_call(
        functools.partial(kernel, n, n_head),
        out_shape=(
            jax.ShapeDtypeStruct((rows, width), bf16),
            jax.ShapeDtypeStruct((far, rows, width), bf16),
        ),
        in_specs=[pl.BlockSpec(memory_space=pltpu.SMEM)] + [hbm] * 5,
        out_specs=(hbm, hbm),
        scratch_shapes=[
            pltpu.VMEM((2, 1, group * half), jnp.int32),
            pltpu.VMEM((rows, HD), f32),
            pltpu.VMEM((rows, HD), f32),
            pltpu.VMEM((rows, depth), bf16),
            pltpu.VMEM((depth, q_cols), bf16),
            pltpu.VMEM((depth, 2 * k_cols), bf16),
            pltpu.VMEM(o_weight.shape, bf16),
            pltpu.VMEM((rows, 2 * k_cols), f32),
            pltpu.VMEM((rows, HD), f32),
            pltpu.VMEM((kv_heads, 2, group * half, HD), bf16),
            pltpu.VMEM((2 * n, kv_heads, half, HD), bf16),
            pltpu.VMEM((2 * n, kv_heads, HD, half), bf16),
            pltpu.VMEM((2 * kv_heads, 1, group * half), f32),
            pltpu.VMEM((2 * kv_heads, 1, group * half), f32),
            pltpu.VMEM((2 * kv_heads, HD, group * half), f32),
            pltpu.VMEM((half, q_cols), bf16),
            pltpu.VMEM((2, tiles, half, tile), f32),
            pltpu.VMEM((2, tiles, half, tile), bf16),
            pltpu.VMEM((2, chips, tiles, half, tile), bf16),
            pltpu.VMEM((2, chips, tiles, half, tile), bf16),
            pltpu.VMEM((2, far, tiles, half, tile), bf16),
            dma((4,)), dma((4,)), dma((4,)), dma, dma,
            dma((1 + n // 2, 2, 2 * n)), dma((2, 2 * n)),
            dma((2, chips, tiles)), dma((2, chips, tiles)),
            dma((2, far, tiles)), dma((2, far, tiles)),
            dma((2, tiles)),
        ],
        compiler_params=pltpu.CompilerParams(
            collective_id=0, has_side_effects=True, vmem_limit_bytes=60 * 2**20
        ),
    )(lengths, tokens, q_weight, k_weight, v_weight, o_weight)
    mixed = near.astype(f32)
    for step in range(chips - 1):
        mixed = mixed + others[step].astype(f32)
    return mixed.astype(bf16)


def solution(mesh):
    return jax.shard_map(
        functools.partial(shards, mesh.shape["ctx"], mesh.shape["head"]),
        mesh=mesh,
        in_specs=(
            P(("groups", "ctx"), None),
            P("groups"),
            P(None, "head"),
            P(None, "head"),
            P(None, "head"),
            P("head", None),
        ),
        out_specs=P(("groups", "ctx"), "head"),
        check_vma=False,
    )
```

```python
import functools
import math

import jax
import jax.numpy as jnp
from jax import lax
from jax.experimental import pallas as pl
from jax.experimental.pallas import tpu as pltpu
from jax.sharding import PartitionSpec as P

HD = 128
MESH = pl.DeviceIdType.MESH
LOW = -1e30


def rotated(values, cosine, sine):
    return values * cosine + pltpu.roll(values, HD // 2, 1) * sine


def kernel(
    n, n_head, lengths_ref, tok_hbm, qw_hbm, kw_hbm, vw_hbm, ow_hbm,
    near_ref, far_ref,
    first_ref, cos_ref, sin_ref, tok, qw, kvw, ow, kv_acc, norm, query, keys, values, top, total, accum, attended,
    kept, sib_out, sib_in, far_out,
    tok_sem, kw_sem, vw_sem, qw_sem, ow_sem,
    kv_send, kv_recv, sib_send, sib_recv, far_send, far_recv,
):
    rows, depth = tok.shape
    half = rows // 2
    kv_heads = keys.shape[1]
    group = query.shape[2] // half
    q_heads = kv_heads * group
    wide_rows = group * half
    k_cols = kv_heads * HD
    chips = n_head // 2
    width = near_ref.shape[1]
    pieces = 4
    piece = depth // pieces

    c = lax.axis_index("ctx")
    head = lax.axis_index("head")
    chip, core = lax.div(head, 2), lax.rem(head, 2)
    sibling = chip * 2 + 1 - core
    has_left, has_right = c > 0, c < n - 1
    low_block, high_block = c, 2 * n - 1 - c

    def other_chip(step):
        return lax.rem(chip + step, chips)

    def load_piece(k):
        cols = pl.ds(pl.multiple_of(k * piece, piece), piece)
        return (
            pltpu.make_async_copy(tok_hbm.at[:, cols], tok.at[:, cols], tok_sem.at[k]),
            pltpu.make_async_copy(kw_hbm.at[cols, :], kvw.at[cols, 0:k_cols], kw_sem.at[k]),
            pltpu.make_async_copy(
                vw_hbm.at[cols, :], kvw.at[cols, k_cols : 2 * k_cols], vw_sem.at[k]
            ),
        )

    for k in range(pieces):
        for copy in load_piece(k):
            copy.start()
    load_q = pltpu.make_async_copy(qw_hbm, qw, qw_sem)
    load_o = pltpu.make_async_copy(ow_hbm, ow, ow_sem)

    barrier = pltpu.get_barrier_semaphore()

    def greet(target):
        pl.semaphore_signal(barrier, inc=1, device_id=target, device_id_type=MESH)

    @pl.when(has_left)
    def _():
        greet({"ctx": c - 1})

    @pl.when(has_right)
    def _():
        greet({"ctx": c + 1})

    greet({"head": sibling})
    for step in range(1, chips):
        greet({"head": other_chip(step) * 2 + core})

    def starts(place):
        first, end = jnp.zeros_like(place), 0
        for d in range(lengths_ref.shape[0]):
            end = end + lengths_ref[d]
            first = jnp.where(place >= end, end, first)
        return first

    for side, block in ((0, low_block), (1, high_block)):
        lane = lax.broadcasted_iota(jnp.int32, (1, half), 1)
        row_first = starts(block * half + lane)
        first_ref[side] = jnp.concatenate([row_first] * group, axis=1)
    lane = lax.broadcasted_iota(jnp.int32, (half, HD), 1)
    on_left = lane < HD // 2
    place = jnp.where(on_left, low_block, high_block) * half + lax.broadcasted_iota(
        jnp.int32, (half, HD), 0
    )
    offset = (place - starts(place)).astype(jnp.float32)
    expo = (lane % (HD // 2)).astype(jnp.float32) * (2.0 / HD)
    angle = offset * jnp.exp(-math.log(500000.0) * expo)
    cosine, sine = jnp.cos(angle), jnp.sin(angle)
    cosine_over, sine_over = pltpu.roll(cosine, HD // 2, 1), pltpu.roll(sine, HD // 2, 1)
    cos_ref[0:half, :] = jnp.where(on_left, cosine, cosine_over)
    cos_ref[half:rows, :] = jnp.where(on_left, cosine_over, cosine)
    sin_ref[0:half, :] = jnp.where(on_left, -sine, sine_over)
    sin_ref[half:rows, :] = jnp.where(on_left, -sine_over, sine)

    kv_acc[...] = jnp.zeros_like(kv_acc)
    norm[...] = jnp.zeros_like(norm)

    def project_piece(k, carry):
        for copy in load_piece(k):
            copy.wait()

        @pl.when(k == pieces // 2)
        def _():
            load_q.start()

        cols = pl.ds(pl.multiple_of(k * piece, piece), piece)

        kv_acc[...] += jnp.dot(tok[:, cols], kvw[cols, :], preferred_element_type=jnp.float32)
        for r in range(0, rows, 64):
            wide = tok[r : r + 64, cols].astype(jnp.float32)
            sq = wide * wide
            part = sq[:, 0:HD]
            for s in range(1, piece // HD):
                part = part + sq[:, s * HD : (s + 1) * HD]
            norm[r : r + 64, :] += part
        return carry

    lax.fori_loop(0, pieces, project_piece, 0)
    mean = jnp.sum(norm[...], axis=1, keepdims=True) * (1.0 / depth)
    norm[...] = jnp.broadcast_to(lax.rsqrt(mean + 1e-05), norm.shape)
    for g in range(kv_heads):
        for side, block in ((0, low_block), (1, high_block)):
            at = slice(side * half, (side + 1) * half)
            raw = kv_acc[at, g * HD : (g + 1) * HD] * norm[at, :]
            keys[block, g] = rotated(raw, cos_ref[at, :], sin_ref[at, :]).astype(jnp.bfloat16)
            raw = kv_acc[at, k_cols + g * HD : k_cols + (g + 1) * HD] * norm[at, :]
            values[block, g] = raw.T.astype(jnp.bfloat16)

    def block_copies(block, way):
        target = {"ctx": c + 2 * way - 1}
        return [
            pltpu.make_async_remote_copy(
                src_ref=ref.at[block],
                dst_ref=ref.at[block],
                send_sem=kv_send.at[way, kind, block],
                recv_sem=kv_recv.at[kind, block],
                device_id=target,
                device_id_type=MESH,
            )
            for kind, ref in enumerate((keys, values))
        ]

    def send(block, way):
        for copy in block_copies(block, way):
            copy.start()

    def receive(block, passes, way):
        landing, onward = block_copies(block, 0), block_copies(block, way)
        for kind in range(2):
            landing[kind].wait_recv()

            @pl.when(passes)
            def _():
                onward[kind].start()

    greeted = 1 + (chips - 1) + has_left.astype(jnp.int32) + has_right.astype(jnp.int32)
    pl.semaphore_wait(barrier, greeted)

    @pl.when(has_left)
    def _():
        send(high_block, 0)

    @pl.when(has_right)
    def _():
        send(low_block, 1)

    load_q.wait()
    load_o.start()
    factor = math.log2(math.e) / math.sqrt(HD)
    tile = min(256, q_heads * HD)

    def project_query(t, carry):
        cols = pl.ds(pl.multiple_of(t * tile, tile), tile)
        raw = jnp.dot(tok[...], qw[:, cols], preferred_element_type=jnp.float32)
        for h in range(tile // HD):
            part = raw[:, h * HD : (h + 1) * HD] * (norm[...] * factor)
            turned = rotated(part, cos_ref[...], sin_ref[...]).astype(jnp.bfloat16)
            at_head = t * (tile // HD) + h
            g, j = lax.div(at_head, group), lax.rem(at_head, group)
            at = pl.ds(pl.multiple_of(j * half, half), half)
            for side in range(2):
                query[g, side, at, :] = turned[side * half : (side + 1) * half]
        return carry

    lax.fori_loop(0, q_heads * HD // tile, project_query, 0)

    def attend(side, block, diagonal):
        def one_group(g, carry):
            slot = side * kv_heads + g
            key_at = lax.broadcasted_iota(jnp.int32, (half, wide_rows), 0)
            allowed = key_at >= first_ref[side] - block * half
            if diagonal:
                row_at = lax.broadcasted_iota(jnp.int32, (1, wide_rows), 1) % half
                allowed = allowed & (key_at <= row_at)
            scores = lax.dot_general(
                keys[block, g], query[g, side], (((1,), (1,)), ((), ())),
                preferred_element_type=jnp.float32,
            )
            scores = jnp.where(allowed, scores, LOW)
            here = jnp.max(scores, axis=0, keepdims=True)
            if not diagonal:
                before = top[slot]
                here = jnp.maximum(before, here)
            expo = jnp.exp2(scores - here)
            summed = jnp.sum(expo, axis=0, keepdims=True)
            fresh = jnp.dot(
                values[block, g], expo.astype(jnp.bfloat16), preferred_element_type=jnp.float32
            )
            if not diagonal:
                shrink = jnp.exp2(before - here)
                summed = summed + total[slot] * shrink
                fresh = fresh + accum[slot] * shrink
            top[slot] = here
            total[slot] = summed
            accum[slot] = fresh
            return carry

        lax.fori_loop(0, kv_heads, one_group, 0)

    def sib_copy(side, x, t):
        return pltpu.make_async_remote_copy(
            src_ref=sib_out.at[side, x, t],
            dst_ref=sib_in.at[side, x, t],
            send_sem=sib_send.at[side, x, t],
            recv_sem=sib_recv.at[side, x, t],
            device_id={"head": sibling},
            device_id_type=MESH,
        )

    def tile_of(side, t):
        cols = pl.ds(pl.multiple_of(t * out_tile, out_tile), out_tile)
        return pl.ds(side * half, half), cols

    def far_copy(side, step, t):
        x = other_chip(step)
        return pltpu.make_async_remote_copy(
            src_ref=far_out.at[side, step - 1, t],
            dst_ref=far_ref.at[step - 1, *tile_of(side, t)],
            send_sem=far_send.at[side, step - 1, t],
            recv_sem=far_recv.at[side, step - 1, t],
            device_id={"head": x * 2 + core},
            device_id_type=MESH,
        )

    out_tile = sib_out.shape[4]
    out_tiles = sib_out.shape[2]

    def project_out(owner, t):
        start = pl.multiple_of(owner * width + t * out_tile, out_tile)
        return jnp.dot(
            attended[...], ow[:, pl.ds(start, out_tile)], preferred_element_type=jnp.float32
        )

    def finish(side):
        for g in range(kv_heads):
            slot = side * kv_heads + g
            result = accum[slot] * (1.0 / total[slot])
            for j in range(group):
                h = g * group + j
                part = result[:, j * half : (j + 1) * half]
                attended[:, h * HD : (h + 1) * HD] = part.T.astype(jnp.bfloat16)
        for step in list(range(1, chips)) + [0]:
            x = other_chip(step)

            def for_sibling(t, carry):
                sib_out[side, x, t] = project_out(x * 2 + 1 - core, t).astype(jnp.bfloat16)
                sib_copy(side, x, t).start()
                return carry

            def for_own(t, carry):
                part = project_out(x * 2 + core, t)
                if step:
                    sib_copy(side, x, t).wait_recv()
                    far_out[side, step - 1, t] = (
                        part + sib_in[side, x, t].astype(jnp.float32)
                    ).astype(jnp.bfloat16)
                    far_copy(side, step, t).start()
                else:
                    kept[side, t] = part
                return carry

            lax.fori_loop(0, out_tiles, for_sibling, 0)
            lax.fori_loop(0, out_tiles, for_own, 0)

    load_o.wait()
    last_right = jnp.maximum(c + 1, n - 1 - c)
    right_count = jnp.where(has_right, 2 * n - 1 - c - last_right, 0)

    def from_left(i):
        return (i >= 1) & (i <= c)

    def from_right(i):
        return (i >= 1) & (i <= right_count)

    def passes_left(i):
        return from_right(i) & has_left & (2 * n - 1 - c - i >= n - c)

    last_pass = jnp.where(has_left, jnp.minimum(right_count, n - 1), 0)
    finish_turn = jnp.maximum(c, jnp.where(c < n - c, last_pass, right_count) - 1)

    def arrive_left(i):
        @pl.when(from_left(i))
        def _():
            receive(c - i, has_right, 1)

    def arrive_right(i):
        @pl.when(from_right(i))
        def _():
            receive(2 * n - 1 - c - i, passes_left(i), 0)

    sends_low = has_left & (c >= n - c)

    @pl.when(sends_low & (right_count == 0))
    def _():
        send(low_block, 0)

    def turn(i, carry):
        @pl.when(passes_left(i + 1))
        def _():
            arrive_right(i + 1)

        @pl.when(from_left(i + 1) & has_right)
        def _():
            arrive_left(i + 1)

        @pl.when(i == 0)
        def _():
            attend(0, low_block, True)
            attend(1, high_block, True)

        @pl.when(from_left(i))
        def _():
            attend(0, c - i, False)

        @pl.when(i == finish_turn)
        def _():
            finish(0)

        @pl.when((i <= c) & (c - i >= n - 1 - c) & (has_right | (i == 0)))
        def _():
            attend(1, c - i, False)

        @pl.when(from_right(i))
        def _():
            attend(1, 2 * n - 1 - c - i, False)

        @pl.when(jnp.logical_not(passes_left(i + 1)))
        def _():
            arrive_right(i + 1)

        @pl.when(sends_low & (i + 1 == right_count))
        def _():
            send(low_block, 0)

        @pl.when(jnp.logical_not(has_right))
        def _():
            arrive_left(i + 1)

        return carry

    lax.fori_loop(0, n + 1, turn, 0)

    @pl.when(jnp.logical_not(has_right))
    def _():
        def put_off(block, carry):
            attend(1, block, False)
            return carry

        lax.fori_loop(0, n - 1, put_off, 0)

    finish(1)

    for side in range(2):

        def add_up(t, carry):
            sib_copy(side, chip, t).wait_recv()
            summed = kept[side, t] + sib_in[side, chip, t].astype(jnp.float32)
            near_ref[tile_of(side, t)] = summed.astype(jnp.bfloat16)
            return carry

        lax.fori_loop(0, out_tiles, add_up, 0)

    def drain_out(t, carry):
        for side in range(2):
            for x in range(chips):
                sib_copy(side, x, t).wait_send()
            for step in range(1, chips):
                far_copy(side, step, t).wait()
        return carry

    lax.fori_loop(0, out_tiles, drain_out, 0)

    def drain(block, carry):
        @pl.when(has_right & (block <= c))
        def _():
            for copy in block_copies(block, 1):
                copy.wait_send()

        @pl.when(has_left & (block >= jnp.maximum(c, n - c)) & (block <= high_block))
        def _():
            for copy in block_copies(block, 0):
                copy.wait_send()

        return carry

    lax.fori_loop(0, 2 * n, drain, 0)


def shards(n, n_head, tokens, lengths, q_weight, k_weight, v_weight, o_weight):
    rows, depth = tokens.shape
    half = rows // 2
    q_cols, k_cols = q_weight.shape[1], k_weight.shape[1]
    q_heads, kv_heads = q_cols // HD, k_cols // HD
    chips = n_head // 2
    width = o_weight.shape[1] // n_head
    group = q_heads // kv_heads
    bf16, f32 = jnp.bfloat16, jnp.float32
    dma = pltpu.SemaphoreType.DMA
    far = max(chips - 1, 1)
    tile = min(256, width)
    tiles = width // tile
    hbm = pl.BlockSpec(memory_space=pl.ANY)
    vmem = pl.BlockSpec(memory_space=pltpu.VMEM)
    near, others = pl.pallas_call(
        functools.partial(kernel, n, n_head),
        out_shape=(
            pltpu.VMEM((rows, width), bf16),
            pltpu.VMEM((far, rows, width), bf16),
        ),
        in_specs=[pl.BlockSpec(memory_space=pltpu.SMEM)] + [hbm] * 5,
        out_specs=(vmem, vmem),
        scratch_shapes=[
            pltpu.VMEM((2, 1, group * half), jnp.int32),
            pltpu.VMEM((rows, HD), f32),
            pltpu.VMEM((rows, HD), f32),
            pltpu.VMEM((rows, depth), bf16),
            pltpu.VMEM((depth, q_cols), bf16),
            pltpu.VMEM((depth, 2 * k_cols), bf16),
            pltpu.VMEM(o_weight.shape, bf16),
            pltpu.VMEM((rows, 2 * k_cols), f32),
            pltpu.VMEM((rows, HD), f32),
            pltpu.VMEM((kv_heads, 2, group * half, HD), bf16),
            pltpu.VMEM((2 * n, kv_heads, half, HD), bf16),
            pltpu.VMEM((2 * n, kv_heads, HD, half), bf16),
            pltpu.VMEM((2 * kv_heads, 1, group * half), f32),
            pltpu.VMEM((2 * kv_heads, 1, group * half), f32),
            pltpu.VMEM((2 * kv_heads, HD, group * half), f32),
            pltpu.VMEM((half, q_cols), bf16),
            pltpu.VMEM((2, tiles, half, tile), f32),
            pltpu.VMEM((2, chips, tiles, half, tile), bf16),
            pltpu.VMEM((2, chips, tiles, half, tile), bf16),
            pltpu.VMEM((2, far, tiles, half, tile), bf16),
            dma((4,)), dma((4,)), dma((4,)), dma, dma,
            dma((2, 2, 2 * n)), dma((2, 2 * n)),
            dma((2, chips, tiles)), dma((2, chips, tiles)),
            dma((2, far, tiles)), dma((2, far, tiles)),
        ],
        compiler_params=pltpu.CompilerParams(
            collective_id=0, has_side_effects=True, vmem_limit_bytes=56 * 2**20
        ),
    )(lengths, tokens, q_weight, k_weight, v_weight, o_weight)
    mixed = near.astype(f32)
    for step in range(chips - 1):
        mixed = mixed + others[step].astype(f32)
    return mixed.astype(bf16)


def solution(mesh):
    return jax.shard_map(
        functools.partial(shards, mesh.shape["ctx"], mesh.shape["head"]),
        mesh=mesh,
        in_specs=(
            P(("groups", "ctx"), None),
            P("groups"),
            P(None, "head"),
            P(None, "head"),
            P(None, "head"),
            P("head", None),
        ),
        out_specs=P(("groups", "ctx"), "head"),
        check_vma=False,
    )
```

```python
import functools
import math

import jax
import jax.numpy as jnp
from jax import lax
from jax.experimental import pallas as pl
from jax.experimental.pallas import tpu as pltpu
from jax.sharding import PartitionSpec as P

HD = 128
MESH = pl.DeviceIdType.MESH
LOW = -1e30


def rotated(values, cosine, sine):
    return values * cosine + pltpu.roll(values, HD // 2, 1) * sine


def kernel(
    n, n_head, lengths_ref, tok_hbm, qw_hbm, kw_hbm, vw_hbm, ow_hbm,
    near_ref, far_ref,
    first_ref, cos_ref, sin_ref, tok, qw, kvw, ow, kv_acc, norm, query, keys, values, top, total, accum, attended,
    kept, sib_out, sib_in, far_out,
    tok_sem, kw_sem, vw_sem, qw_sem, ow_sem,
    kv_send, kv_recv, sib_send, sib_recv, far_send, far_recv,
):
    rows, depth = tok.shape
    half = rows // 2
    kv_heads = keys.shape[1]
    group = query.shape[2] // half
    q_heads = kv_heads * group
    wide_rows = group * half
    k_cols = kv_heads * HD
    chips = n_head // 2
    width = near_ref.shape[1]
    pieces = 4
    piece = depth // pieces

    c = lax.axis_index("ctx")
    head = lax.axis_index("head")
    chip, core = lax.div(head, 2), lax.rem(head, 2)
    sibling = chip * 2 + 1 - core
    has_left, has_right = c > 0, c < n - 1
    low_block, high_block = c, 2 * n - 1 - c

    def other_chip(step):
        return lax.rem(chip + step, chips)

    def load_piece(k):
        cols = pl.ds(pl.multiple_of(k * piece, piece), piece)
        return (
            pltpu.make_async_copy(tok_hbm.at[:, cols], tok.at[:, cols], tok_sem.at[k]),
            pltpu.make_async_copy(kw_hbm.at[cols, :], kvw.at[cols, 0:k_cols], kw_sem.at[k]),
            pltpu.make_async_copy(
                vw_hbm.at[cols, :], kvw.at[cols, k_cols : 2 * k_cols], vw_sem.at[k]
            ),
        )

    for k in range(pieces):
        for copy in load_piece(k):
            copy.start()
    load_q = pltpu.make_async_copy(qw_hbm, qw, qw_sem)
    load_o = pltpu.make_async_copy(ow_hbm, ow, ow_sem)

    barrier = pltpu.get_barrier_semaphore()

    def greet(target):
        pl.semaphore_signal(barrier, inc=1, device_id=target, device_id_type=MESH)

    @pl.when(has_left)
    def _():
        greet({"ctx": c - 1})

    @pl.when(has_right)
    def _():
        greet({"ctx": c + 1})

    greet({"head": sibling})
    for step in range(1, chips):
        greet({"head": other_chip(step) * 2 + core})

    def starts(place):
        first, end = jnp.zeros_like(place), 0
        for d in range(lengths_ref.shape[0]):
            end = end + lengths_ref[d]
            first = jnp.where(place >= end, end, first)
        return first

    for side, block in ((0, low_block), (1, high_block)):
        lane = lax.broadcasted_iota(jnp.int32, (1, half), 1)
        row_first = starts(block * half + lane)
        first_ref[side] = jnp.concatenate([row_first] * group, axis=1)
    lane = lax.broadcasted_iota(jnp.int32, (half, HD), 1)
    on_left = lane < HD // 2
    place = jnp.where(on_left, low_block, high_block) * half + lax.broadcasted_iota(
        jnp.int32, (half, HD), 0
    )
    offset = (place - starts(place)).astype(jnp.float32)
    expo = (lane % (HD // 2)).astype(jnp.float32) * (2.0 / HD)
    angle = offset * jnp.exp(-math.log(500000.0) * expo)
    cosine, sine = jnp.cos(angle), jnp.sin(angle)
    cosine_over, sine_over = pltpu.roll(cosine, HD // 2, 1), pltpu.roll(sine, HD // 2, 1)
    cos_ref[0:half, :] = jnp.where(on_left, cosine, cosine_over)
    cos_ref[half:rows, :] = jnp.where(on_left, cosine_over, cosine)
    sin_ref[0:half, :] = jnp.where(on_left, -sine, sine_over)
    sin_ref[half:rows, :] = jnp.where(on_left, -sine_over, sine)

    kv_acc[...] = jnp.zeros_like(kv_acc)
    norm[...] = jnp.zeros_like(norm)

    def project_side(side, block):
        at = slice(side * half, (side + 1) * half)

        def project_piece(k, carry):
            if side == 0:
                for copy in load_piece(k):
                    copy.wait()

                @pl.when(k == pieces // 2)
                def _():
                    load_q.start()

            cols = pl.ds(pl.multiple_of(k * piece, piece), piece)
            kv_acc[at, :] += jnp.dot(
                tok[at, cols], kvw[cols, :], preferred_element_type=jnp.float32
            )
            for r in range(side * half, (side + 1) * half, 64):
                wide = tok[r : r + 64, cols].astype(jnp.float32)
                sq = wide * wide
                part = sq[:, 0:HD]
                for s in range(1, piece // HD):
                    part = part + sq[:, s * HD : (s + 1) * HD]
                norm[r : r + 64, :] += part
            return carry

        lax.fori_loop(0, pieces, project_piece, 0)
        mean = jnp.sum(norm[at, :], axis=1, keepdims=True) * (1.0 / depth)
        norm[at, :] = jnp.broadcast_to(lax.rsqrt(mean + 1e-05), (half, HD))
        for g in range(kv_heads):
            raw = kv_acc[at, g * HD : (g + 1) * HD] * norm[at, :]
            keys[block, g] = rotated(raw, cos_ref[at, :], sin_ref[at, :]).astype(jnp.bfloat16)
            raw = kv_acc[at, k_cols + g * HD : k_cols + (g + 1) * HD] * norm[at, :]
            values[block, g] = raw.T.astype(jnp.bfloat16)

    def block_copies(block, way):
        target = {"ctx": c + 2 * way - 1}
        return [
            pltpu.make_async_remote_copy(
                src_ref=ref.at[block],
                dst_ref=ref.at[block],
                send_sem=kv_send.at[way, kind, block],
                recv_sem=kv_recv.at[kind, block],
                device_id=target,
                device_id_type=MESH,
            )
            for kind, ref in enumerate((keys, values))
        ]

    def send(block, way):
        for copy in block_copies(block, way):
            copy.start()

    def receive(block, passes, way):
        landing, onward = block_copies(block, 0), block_copies(block, way)
        for kind in range(2):
            landing[kind].wait_recv()

            @pl.when(passes)
            def _():
                onward[kind].start()

    greeted = 1 + (chips - 1) + has_left.astype(jnp.int32) + has_right.astype(jnp.int32)

    project_side(0, low_block)
    pl.semaphore_wait(barrier, greeted)

    @pl.when(has_right)
    def _():
        send(low_block, 1)

    project_side(1, high_block)

    @pl.when(has_left)
    def _():
        send(high_block, 0)

    load_q.wait()
    load_o.start()
    factor = math.log2(math.e) / math.sqrt(HD)
    tile = min(256, q_heads * HD)

    def project_query(t, carry):
        cols = pl.ds(pl.multiple_of(t * tile, tile), tile)
        raw = jnp.dot(tok[...], qw[:, cols], preferred_element_type=jnp.float32)
        for h in range(tile // HD):
            part = raw[:, h * HD : (h + 1) * HD] * (norm[...] * factor)
            turned = rotated(part, cos_ref[...], sin_ref[...]).astype(jnp.bfloat16)
            at_head = t * (tile // HD) + h
            g, j = lax.div(at_head, group), lax.rem(at_head, group)
            at = pl.ds(pl.multiple_of(j * half, half), half)
            for side in range(2):
                query[g, side, at, :] = turned[side * half : (side + 1) * half]
        return carry

    lax.fori_loop(0, q_heads * HD // tile, project_query, 0)

    def attend(side, block, diagonal):
        def one_group(g, carry):
            slot = side * kv_heads + g
            key_at = lax.broadcasted_iota(jnp.int32, (half, wide_rows), 0)
            allowed = key_at >= first_ref[side] - block * half
            if diagonal:
                row_at = lax.broadcasted_iota(jnp.int32, (1, wide_rows), 1) % half
                allowed = allowed & (key_at <= row_at)
            scores = lax.dot_general(
                keys[block, g], query[g, side], (((1,), (1,)), ((), ())),
                preferred_element_type=jnp.float32,
            )
            scores = jnp.where(allowed, scores, LOW)
            here = jnp.max(scores, axis=0, keepdims=True)
            if not diagonal:
                before = top[slot]
                here = jnp.maximum(before, here)
            expo = jnp.exp2(scores - here)
            summed = jnp.sum(expo, axis=0, keepdims=True)
            fresh = jnp.dot(
                values[block, g], expo.astype(jnp.bfloat16), preferred_element_type=jnp.float32
            )
            if not diagonal:
                shrink = jnp.exp2(before - here)
                summed = summed + total[slot] * shrink
                fresh = fresh + accum[slot] * shrink
            top[slot] = here
            total[slot] = summed
            accum[slot] = fresh
            return carry

        lax.fori_loop(0, kv_heads, one_group, 0)

    def sib_copy(side, x, t):
        return pltpu.make_async_remote_copy(
            src_ref=sib_out.at[side, x, t],
            dst_ref=sib_in.at[side, x, t],
            send_sem=sib_send.at[side, x, t],
            recv_sem=sib_recv.at[side, x, t],
            device_id={"head": sibling},
            device_id_type=MESH,
        )

    def tile_of(side, t):
        cols = pl.ds(pl.multiple_of(t * out_tile, out_tile), out_tile)
        return pl.ds(side * half, half), cols

    def far_copy(side, step, t):
        x = other_chip(step)
        return pltpu.make_async_remote_copy(
            src_ref=far_out.at[side, step - 1, t],
            dst_ref=far_ref.at[step - 1, *tile_of(side, t)],
            send_sem=far_send.at[side, step - 1, t],
            recv_sem=far_recv.at[side, step - 1, t],
            device_id={"head": x * 2 + core},
            device_id_type=MESH,
        )

    out_tile = sib_out.shape[4]
    out_tiles = sib_out.shape[2]

    def project_out(owner, t):
        start = pl.multiple_of(owner * width + t * out_tile, out_tile)
        return jnp.dot(
            attended[...], ow[:, pl.ds(start, out_tile)], preferred_element_type=jnp.float32
        )

    def finish(side):
        for g in range(kv_heads):
            slot = side * kv_heads + g
            result = accum[slot] * (1.0 / total[slot])
            for j in range(group):
                h = g * group + j
                part = result[:, j * half : (j + 1) * half]
                attended[:, h * HD : (h + 1) * HD] = part.T.astype(jnp.bfloat16)
        for step in list(range(1, chips)) + [0]:
            x = other_chip(step)

            def for_sibling(t, carry):
                sib_out[side, x, t] = project_out(x * 2 + 1 - core, t).astype(jnp.bfloat16)
                sib_copy(side, x, t).start()
                return carry

            def for_own(t, carry):
                part = project_out(x * 2 + core, t)
                if step:
                    sib_copy(side, x, t).wait_recv()
                    far_out[side, step - 1, t] = (
                        part + sib_in[side, x, t].astype(jnp.float32)
                    ).astype(jnp.bfloat16)
                    far_copy(side, step, t).start()
                else:
                    kept[side, t] = part
                return carry

            lax.fori_loop(0, out_tiles, for_sibling, 0)
            lax.fori_loop(0, out_tiles, for_own, 0)

    load_o.wait()
    last_right = jnp.maximum(c + 1, n - 1 - c)
    right_count = jnp.where(has_right, 2 * n - 1 - c - last_right, 0)

    def from_left(i):
        return (i >= 1) & (i <= c)

    def from_right(i):
        return (i >= 1) & (i <= right_count)

    def passes_left(i):
        return from_right(i) & has_left & (2 * n - 1 - c - i >= n - c)

    last_pass = jnp.where(has_left, jnp.minimum(right_count, n - 1), 0)
    finish_turn = jnp.maximum(c, jnp.where(c < n - c, last_pass, right_count) - 1)

    def arrive_left(i):
        @pl.when(from_left(i))
        def _():
            receive(c - i, has_right, 1)

    def arrive_right(i):
        @pl.when(from_right(i))
        def _():
            receive(2 * n - 1 - c - i, passes_left(i), 0)

    sends_low = has_left & (c >= n - c)

    @pl.when(sends_low & (right_count == 0))
    def _():
        send(low_block, 0)

    def turn(i, carry):
        @pl.when(passes_left(i + 1))
        def _():
            arrive_right(i + 1)

        @pl.when(from_left(i + 1) & has_right)
        def _():
            arrive_left(i + 1)

        @pl.when(i == 0)
        def _():
            attend(0, low_block, True)
            attend(1, high_block, True)

        @pl.when(from_left(i))
        def _():
            attend(0, c - i, False)

        @pl.when(i == finish_turn)
        def _():
            finish(0)

        @pl.when((i <= c) & (c - i >= n - 1 - c) & (has_right | (i == 0)))
        def _():
            attend(1, c - i, False)

        @pl.when(from_right(i))
        def _():
            attend(1, 2 * n - 1 - c - i, False)

        @pl.when(jnp.logical_not(passes_left(i + 1)))
        def _():
            arrive_right(i + 1)

        @pl.when(sends_low & (i + 1 == right_count))
        def _():
            send(low_block, 0)

        @pl.when(jnp.logical_not(has_right))
        def _():
            arrive_left(i + 1)

        return carry

    lax.fori_loop(0, n + 1, turn, 0)

    @pl.when(jnp.logical_not(has_right))
    def _():
        def put_off(block, carry):
            attend(1, block, False)
            return carry

        lax.fori_loop(0, n - 1, put_off, 0)

    finish(1)

    for side in range(2):

        def add_up(t, carry):
            sib_copy(side, chip, t).wait_recv()
            summed = kept[side, t] + sib_in[side, chip, t].astype(jnp.float32)
            near_ref[tile_of(side, t)] = summed.astype(jnp.bfloat16)
            return carry

        lax.fori_loop(0, out_tiles, add_up, 0)

    def drain_out(t, carry):
        for side in range(2):
            for x in range(chips):
                sib_copy(side, x, t).wait_send()
            for step in range(1, chips):
                far_copy(side, step, t).wait()
        return carry

    lax.fori_loop(0, out_tiles, drain_out, 0)

    def drain(block, carry):
        @pl.when(has_right & (block <= c))
        def _():
            for copy in block_copies(block, 1):
                copy.wait_send()

        @pl.when(has_left & (block >= jnp.maximum(c, n - c)) & (block <= high_block))
        def _():
            for copy in block_copies(block, 0):
                copy.wait_send()

        return carry

    lax.fori_loop(0, 2 * n, drain, 0)


def shards(n, n_head, tokens, lengths, q_weight, k_weight, v_weight, o_weight):
    rows, depth = tokens.shape
    half = rows // 2
    q_cols, k_cols = q_weight.shape[1], k_weight.shape[1]
    q_heads, kv_heads = q_cols // HD, k_cols // HD
    chips = n_head // 2
    width = o_weight.shape[1] // n_head
    group = q_heads // kv_heads
    bf16, f32 = jnp.bfloat16, jnp.float32
    dma = pltpu.SemaphoreType.DMA
    far = max(chips - 1, 1)
    tile = min(256, width)
    tiles = width // tile
    hbm = pl.BlockSpec(memory_space=pl.ANY)
    vmem = pl.BlockSpec(memory_space=pltpu.VMEM)
    near, others = pl.pallas_call(
        functools.partial(kernel, n, n_head),
        out_shape=(
            pltpu.VMEM((rows, width), bf16),
            pltpu.VMEM((far, rows, width), bf16),
        ),
        in_specs=[pl.BlockSpec(memory_space=pltpu.SMEM)] + [hbm] * 5,
        out_specs=(vmem, vmem),
        scratch_shapes=[
            pltpu.VMEM((2, 1, group * half), jnp.int32),
            pltpu.VMEM((rows, HD), f32),
            pltpu.VMEM((rows, HD), f32),
            pltpu.VMEM((rows, depth), bf16),
            pltpu.VMEM((depth, q_cols), bf16),
            pltpu.VMEM((depth, 2 * k_cols), bf16),
            pltpu.VMEM(o_weight.shape, bf16),
            pltpu.VMEM((rows, 2 * k_cols), f32),
            pltpu.VMEM((rows, HD), f32),
            pltpu.VMEM((kv_heads, 2, group * half, HD), bf16),
            pltpu.VMEM((2 * n, kv_heads, half, HD), bf16),
            pltpu.VMEM((2 * n, kv_heads, HD, half), bf16),
            pltpu.VMEM((2 * kv_heads, 1, group * half), f32),
            pltpu.VMEM((2 * kv_heads, 1, group * half), f32),
            pltpu.VMEM((2 * kv_heads, HD, group * half), f32),
            pltpu.VMEM((half, q_cols), bf16),
            pltpu.VMEM((2, tiles, half, tile), f32),
            pltpu.VMEM((2, chips, tiles, half, tile), bf16),
            pltpu.VMEM((2, chips, tiles, half, tile), bf16),
            pltpu.VMEM((2, far, tiles, half, tile), bf16),
            dma((4,)), dma((4,)), dma((4,)), dma, dma,
            dma((2, 2, 2 * n)), dma((2, 2 * n)),
            dma((2, chips, tiles)), dma((2, chips, tiles)),
            dma((2, far, tiles)), dma((2, far, tiles)),
        ],
        compiler_params=pltpu.CompilerParams(
            collective_id=0, has_side_effects=True, vmem_limit_bytes=56 * 2**20
        ),
    )(lengths, tokens, q_weight, k_weight, v_weight, o_weight)
    mixed = near.astype(f32)
    for step in range(chips - 1):
        mixed = mixed + others[step].astype(f32)
    return mixed.astype(bf16)


def solution(mesh):
    return jax.shard_map(
        functools.partial(shards, mesh.shape["ctx"], mesh.shape["head"]),
        mesh=mesh,
        in_specs=(
            P(("groups", "ctx"), None),
            P("groups"),
            P(None, "head"),
            P(None, "head"),
            P(None, "head"),
            P("head", None),
        ),
        out_specs=P(("groups", "ctx"), "head"),
        check_vma=False,
    )
```
